256 devices in a mesh: space: 8 (over y, core), vel: 32 (over z, x).
Axes of the slice: x: 4, y: 4, z: 8, core: 2. Of those that a mesh axis runs over, the one named last changes fastest.
Arguments:
- distribution: float32 [8, 256, 13824], P('space', None, 'vel'), may hold values from -6 to 6
- neighbours: int32 [8, 4], P('space'), may hold values from -1 to 7, as said below
- block_level: int32 [8], P('space'), may hold values from 0 to 2
- collide_mask: int32 [2048], P('space'), may hold values from 0 to 1, as said below
- gain_first: float32 [6, 13824], replicated, may hold values from -1.8 to 1.8
- gain_second: float32 [6, 13824], replicated, may hold values from -1.8 to 1.8
- loss_rates: float32 [13824], replicated, may hold values from 0.2 to 2
Outputs:
- distribution_next: float32 [8, 256, 13824], P('space', None, 'vel')
The draws below stay inside these ranges and needn't reach their ends.
Inputs may be any that keep to these rules, and one draw needn't show every extreme that they name: `neighbours`: each entry is -1 or a block held by the same index of space as the block itself or by the index one below or one above (index s holds blocks s * 1 to (s + 1) - 1). `collide_mask`: the cells of one index of space (its 1 block) hold at most 128 ones, and some index holds exactly 128.
All inputs are finite; a program needn't handle non-finite values.
Results may differ from the reference program's by a relative error of at most 0.0003.
Values sent between devices are 32-bit elements; how exact they have to be, the bound alone decides.
No kernel may reach another device: no remote copies, remote signals or barrier semaphores. Data moves between devices by JAX's collectives and lax.ppermute only.
A program may use at most 128 MiB of HBM per device.

```python
import math
import jax
import jax.numpy as jnp
from jax import lax

BSIDE = 16
VDIM = 24
TERMS = 6
LEVELS = 3
BLK_DEV = 1
NB = 8
ACT = 128
NV = 13824


def draw_neighbours(key, part):
    spaces = NB // BLK_DEV
    blocks = jnp.arange(NB, dtype=jnp.int32)
    owner_index = blocks // BLK_DEV
    key_kind, key_within = jax.random.split(jax.random.fold_in(key, 11), 2)
    face_kind = jax.random.randint(key_kind, (NB, 4), 0, 8)
    offset = jnp.where(face_kind <= 2, -1, jnp.where(face_kind <= 5, 0, 1))
    first_block = (blocks % BLK_DEV == 0) & (owner_index > 0)
    final_block = (blocks % BLK_DEV == BLK_DEV - 1) & (owner_index < spaces - 1)
    offset = offset.at[:, 2].set(jnp.where(first_block, -1, offset[:, 2]))
    offset = offset.at[:, 3].set(jnp.where(final_block, 1, offset[:, 3]))
    face_kind = face_kind.at[:, 2].set(jnp.where(first_block, 1, face_kind[:, 2]))
    face_kind = face_kind.at[:, 3].set(jnp.where(final_block, 7, face_kind[:, 3]))
    target = owner_index[:, None] + offset
    within = jax.random.randint(key_within, (NB, 4), 0, BLK_DEV)
    source = target * BLK_DEV + within
    usable = (face_kind != 0) & (target >= 0) & (target < spaces)
    source = jnp.where(usable, source, -1)
    source = source.at[0, 0].set(-1)
    source = source.at[NB - 2, 1].set(NB - 1)
    return source.astype(jnp.int32)


def draw_collide_mask(key, part):
    spaces = NB // BLK_DEV
    per_space = BLK_DEV * BSIDE * BSIDE
    key_count, key_full, key_order = jax.random.split(jax.random.fold_in(key, 23), 3)
    counts = jax.random.randint(key_count, (spaces,), ACT // 2, ACT + 1)
    busiest = jax.random.randint(key_full, (), 0, spaces)
    counts = counts.at[busiest].set(ACT)

    def one_order(single):
        return jax.random.permutation(single, per_space)
    orders = jax.vmap(one_order)(jax.random.split(key_order, spaces))
    return (orders < counts[:, None]).astype(jnp.int32).reshape(-1)


def set_ends(array, rng, least, top_value):
    longest = array.shape.index(max(array.shape))
    spots = []
    for shift in (0, 1):
        where = [jax.random.randint(jax.random.fold_in(rng, axis), (), 0, length) for axis, length in enumerate(array.shape)]
        where[longest] = (where[longest] + shift) % array.shape[longest]
        spots.append(tuple(where))
    return array.at[spots[0]].set(least).at[spots[1]].set(top_value)


def shard_levels(stream_key, shape, cuts, low, largest):
    level, own = 1.0, jax.random.fold_in(stream_key, 6)
    for position, shards_of in cuts:
        steps = jnp.exp(jax.random.uniform(jax.random.fold_in(own, position), (shards_of,), jnp.float32, low / len(cuts), largest / len(cuts)))
        level = level * jnp.repeat(steps, shape[position] // shards_of).reshape([-1 if axis == position else 1 for axis in range(len(shape))])
    return level


def bell_draw(own_key, shape, spread, limit, cuts=(), kind=jnp.bfloat16):
    values = jax.random.normal(own_key, shape, jnp.float32) * spread
    if len(cuts) > 0:
        values = shard_levels(own_key, shape, cuts, -0.22, 0.18) * values
    return jnp.clip(values, min=-limit, max=limit).astype(kind)


def setup_inputs(seed: int = 0) -> dict:
    key_list = jax.random.split(jax.random.key(seed), 8)
    distribution = bell_draw(key_list[0], (NB, BSIDE * BSIDE, NV), 1.0, 6.0, ((0, 8), (2, 32)), jnp.float32)
    neighbours = draw_neighbours(jax.random.fold_in(key_list[7], 71), 0)
    block_level = set_ends(jax.random.randint(key_list[2], (NB,), 0, LEVELS), jax.random.fold_in(key_list[2], 1), 0, LEVELS - 1).astype(jnp.int32)
    collide_mask = draw_collide_mask(jax.random.fold_in(key_list[7], 71), 0)
    gain_first = bell_draw(key_list[4], (TERMS, NV), 0.3, 1.8, (), jnp.float32)
    gain_second = bell_draw(key_list[5], (TERMS, NV), 0.3, 1.8, (), jnp.float32)
    loss_rates = jnp.clip(jnp.exp(jax.random.uniform(key_list[6], (NV,), jnp.float32, math.log(0.2), math.log(2.0))), 0.2, 2.0)
    return dict(distribution=distribution, neighbours=neighbours, block_level=block_level, collide_mask=collide_mask, gain_first=gain_first, gain_second=gain_second, loss_rates=loss_rates)


weno_eps = 1e-06
courant = 0.2

def weno_value(minus_two, minus_one, middle, plus_one, plus_two):
    guess_low = (2.0 * minus_two - 7.0 * minus_one + 11.0 * middle) / 6.0
    guess_mid = (-minus_one + 5.0 * middle + 2.0 * plus_one) / 6.0
    guess_high = (2.0 * middle + 5.0 * plus_one - plus_two) / 6.0
    rough_low = 13.0 / 12.0 * (minus_two - 2.0 * minus_one + middle) ** 2 + 0.25 * (minus_two - 4.0 * minus_one + 3.0 * middle) ** 2
    rough_mid = 13.0 / 12.0 * (minus_one - 2.0 * middle + plus_one) ** 2 + 0.25 * (minus_one - plus_one) ** 2
    rough_high = 13.0 / 12.0 * (middle - 2.0 * plus_one + plus_two) ** 2 + 0.25 * (3.0 * middle - 4.0 * plus_one + plus_two) ** 2
    weight_low = 0.1 / (weno_eps + rough_low) ** 2
    weight_mid = 0.6 / (weno_eps + rough_mid) ** 2
    weight_high = 0.3 / (weno_eps + rough_high) ** 2
    return (weight_low * guess_low + weight_mid * guess_mid + weight_high * guess_high) / (weight_low + weight_mid + weight_high)

def edge_values(padded, along, cell_count):

    def shifted(offset):
        return lax.slice_in_dim(padded, offset, offset + cell_count + 1, axis=along)
    upwind_low = weno_value(shifted(0), shifted(1), shifted(2), shifted(3), shifted(4))
    upwind_high = weno_value(shifted(5), shifted(4), shifted(3), shifted(2), shifted(1))
    return (upwind_low, upwind_high)

def flux_change(padded, along, cell_count, velocity):
    from_low, from_high = edge_values(padded, along, cell_count)
    step_low = lax.slice_in_dim(from_low, 1, cell_count + 1, axis=along) - lax.slice_in_dim(from_low, 0, cell_count, axis=along)
    step_high = lax.slice_in_dim(from_high, 1, cell_count + 1, axis=along) - lax.slice_in_dim(from_high, 0, cell_count, axis=along)
    return jnp.maximum(velocity, 0.0) * step_low + jnp.minimum(velocity, 0.0) * step_high

def transport_rate(padded_first, padded_second, along, cell_count, speed_first, speed_second, courant_ratio):
    change = flux_change(padded_first, along, cell_count, speed_first) + flux_change(padded_second, along + 1, cell_count, speed_second)
    return -courant_ratio * change

def grid_speeds(vel_start, vel_width, vdim):
    index = vel_start + jnp.arange(vel_width, dtype=jnp.int32)
    first_index = index // (vdim * vdim)
    second_index = index // vdim % vdim
    half = (vdim - 1) / 2.0
    return ((first_index.astype(jnp.float32) - half) / half, (second_index.astype(jnp.float32) - half) / half)

def hartley(length):
    grid_index = jnp.arange(length, dtype=jnp.float32)
    angle_table = 2.0 * jnp.pi * grid_index[:, None] * grid_index[None, :] / length
    return (jnp.cos(angle_table) + jnp.sin(angle_table)) / jnp.sqrt(jnp.float32(length))

def hartley_cube(velocity_cube, hartley_table):
    highest = lax.Precision.HIGHEST
    velocity_cube = jnp.einsum('cijk,kl->cijl', velocity_cube, hartley_table, precision=highest)
    velocity_cube = jnp.einsum('cijk,jl->cilk', velocity_cube, hartley_table, precision=highest)
    return jnp.einsum('cijk,il->cljk', velocity_cube, hartley_table, precision=highest)

def collide(cell_rows, gain_first, gain_second, loss_rates, hartley_table):
    row_count = cell_rows.shape[0]
    vdim = hartley_table.shape[0]
    velocity_cube = cell_rows.reshape(row_count, vdim, vdim, vdim)
    spectrum = hartley_cube(velocity_cube, hartley_table)
    gain_total = jnp.zeros_like(velocity_cube)
    for term_index in range(gain_first.shape[0]):
        gain_one = hartley_cube(spectrum * gain_first[term_index].reshape(vdim, vdim, vdim), hartley_table)
        gain_two = hartley_cube(spectrum * gain_second[term_index].reshape(vdim, vdim, vdim), hartley_table)
        gain_total = gain_total + gain_one * gain_two
    loss_part = hartley_cube(spectrum * loss_rates.reshape(vdim, vdim, vdim), hartley_table)
    return (gain_total - velocity_cube * loss_part).reshape(row_count, -1)

def block_rates(density, neighbours, block_level, speed_first, speed_second):
    block_side = density.shape[1]

    def one_block(block_index):
        own_block = density[block_index]
        sources = neighbours[block_index]

        def ghost(face_index):
            source = sources[face_index]
            return density[jnp.maximum(source, 0)] * (source >= 0).astype(jnp.float32)
        ghost_west = ghost(0)[block_side - 3:]
        ghost_east = ghost(1)[:3]
        ghost_south = ghost(2)[:, block_side - 3:]
        ghost_north = ghost(3)[:, :3]
        padded_first = jnp.concatenate([ghost_west, own_block, ghost_east], axis=0)
        padded_second = jnp.concatenate([ghost_south, own_block, ghost_north], axis=1)
        courant_ratio = courant * jnp.exp2(block_level[block_index].astype(jnp.float32))
        return transport_rate(padded_first, padded_second, 0, block_side, speed_first, speed_second, courant_ratio)
    return lax.map(one_block, jnp.arange(NB, dtype=jnp.int32))

def reference(distribution, neighbours, block_level, collide_mask, gain_first, gain_second, loss_rates):
    density = distribution.reshape(NB, BSIDE, BSIDE, NV)
    speed_first, speed_second = grid_speeds(0, NV, VDIM)
    section_one = density + block_rates(density, neighbours, block_level, speed_first, speed_second)
    section_two = 0.5 * density + 0.5 * (section_one + block_rates(section_one, neighbours, block_level, speed_first, speed_second))
    hartley_table = hartley(VDIM)
    flat_cells = section_two.reshape(NB, BSIDE * BSIDE, NV)
    marked = collide_mask.reshape(NB, BSIDE * BSIDE).astype(jnp.float32)

    def collide_block(inputs):
        cell_rows, block_marks = inputs
        return cell_rows + block_marks[:, None] * collide(cell_rows, gain_first, gain_second, loss_rates, hartley_table)
    return lax.map(collide_block, (flat_cells, marked))
```

```python
import jax
import jax.numpy as jnp
import ml_dtypes
import numpy as np
from jax import lax
from jax.experimental import pallas as pl
from jax.experimental.pallas import tpu as pltpu
from jax.sharding import PartitionSpec as P

BSIDE = 16
VDIM = 24
CELLS = BSIDE * BSIDE
TERMS = 6
ACT = 128
LANES = 128
WIDTH = 432
TILES = 4
TAIL = WIDTH - 3 * LANES
GROUP = 32
OWN = ACT // GROUP
CHUNK = TILES * OWN
PLANE = VDIM * VDIM
EDGE = 5 * BSIDE
COURANT = 0.2
EPS = 1e-06

f32 = jnp.float32
bf16 = jnp.bfloat16


def hartley_pieces():
    k = np.arange(VDIM)
    angle = 2.0 * np.pi * ((k[:, None] * k[None, :]) % VDIM) / VDIM
    table = (np.cos(angle) + np.sin(angle)) / np.sqrt(VDIM)
    place = np.arange(VDIM)
    first = 3 * (place % 8) + place // 8

    def pieces(array):
        high = array.astype(ml_dtypes.bfloat16)
        low = (array - high.astype(np.float64)).astype(ml_dtypes.bfloat16)
        return jnp.asarray(high), jnp.asarray(low)

    plane = np.kron(table, table)
    forward = np.kron(np.eye(OWN), table[:, first])
    back = np.kron(np.eye(2 * OWN), table[first, :])
    return (*pieces(plane), *pieces(forward), *pieces(back))


def dot(a, b):
    return jnp.dot(a, b, preferred_element_type=f32)


def split(a):
    high = a.astype(bf16)
    return high, (a - high.astype(f32)).astype(bf16)


def product(a, b):
    return dot(a[0], b[0]) + dot(a[1], b[0]) + dot(a[0], b[1])


def velocity_lanes(tile):
    start = lax.axis_index("vel") * WIDTH + tile * LANES
    lane = lax.broadcasted_iota(jnp.int32, (8, LANES), 1)
    g = (start + lane).astype(f32)
    rows = jnp.floor((g + 0.5) * (1.0 / VDIM))
    first = jnp.floor((rows + 0.5) * (1.0 / VDIM))
    second = rows - VDIM * first
    half = (VDIM - 1) / 2.0
    return (first - half) / half, (second - half) / half


def upwind_steps(u):
    count = BSIDE
    d = [u[m + 1] - u[m] for m in range(count + 4)]
    low, mid, high, rise, fall, side = {}, {}, {}, {}, {}, {}
    twice = [a + a for a in d]
    for m in range(count + 3):
        left, right = d[m], d[m + 1]
        bend = right - left
        base = bend * bend * (13.0 / 3.0) + 4.0 * EPS
        rise[m] = twice[m + 1] + bend
        side[m] = left + right
        fall[m] = bend - twice[m]
        if m <= count:
            t = base + rise[m] * rise[m]
            low[m] = t * t
        if 1 <= m <= count + 1:
            t = base + side[m] * side[m]
            mid[m] = t * t
        if m >= 2:
            t = base + fall[m] * fall[m]
            high[m] = t * t
    values = []
    for i in range(count + 1):
        s0, s1, s2 = low[i], mid[i + 1], high[i + 2]
        d1, d2 = d[i + 1], d[i + 2]
        w0 = s1 * s2 * (1.0 / 3.0)
        w1 = s0 * s2 * 2.0
        w2 = s0 * s1
        p0 = rise[i] + rise[i] - d1
        p1 = side[i + 1] + d2
        p2 = d2 - fall[i + 2]
        top = w0 * p0 + w1 * p1 + w2 * p2
        values.append(u[i + 2] + top / (6.0 * (w0 + w1 + w2)))
    return [values[i + 1] - values[i] for i in range(count)]


def along(cells, lower, upper, neg, speed):
    wind = [jnp.where(neg, cells[BSIDE - 1 - i], cells[i]) for i in range(BSIDE)]
    u = [
        jnp.where(neg, upper[4], lower[4]),
        jnp.where(neg, upper[1], lower[2]),
        jnp.where(neg, upper[0], lower[3]),
        *wind,
        jnp.where(neg, lower[3], upper[0]),
        jnp.where(neg, lower[2], upper[1]),
    ]
    steps = [speed * s for s in upwind_steps(u)]
    return [jnp.where(neg, steps[BSIDE - 1 - i], steps[i]) for i in range(BSIDE)]


def row_cells(ref, tile, i, half):
    return ref[tile, i * BSIDE + 8 * half : i * BSIDE + 8 * half + 8, :]


def column_place(j, half):
    return pl.ds(8 * half * BSIDE + j, 8, stride=BSIDE)


def write_edges(cells_ref, edge_ref):
    for tile in range(TILES):
        first, second = velocity_lanes(tile)
        for half in range(2):
            for layer, i in enumerate((0, 1, 14, 15, None)):
                if i is None:
                    a = jnp.where(first < 0, row_cells(cells_ref, tile, 2, half), row_cells(cells_ref, tile, 13, half))
                    b = jnp.where(
                        second < 0,
                        cells_ref[tile, column_place(2, half), :],
                        cells_ref[tile, column_place(13, half), :],
                    )
                else:
                    a = row_cells(cells_ref, tile, i, half)
                    b = cells_ref[tile, column_place(i, half), :]
                at = layer * BSIDE + 8 * half
                if tile < TILES - 1:
                    base = tile * 2 * EDGE
                    edge_ref[base + at : base + at + 8, :] = a
                    edge_ref[base + EDGE + at : base + EDGE + at + 8, :] = b
                else:
                    base = tile * 2 * EDGE
                    lane = lax.broadcasted_iota(jnp.int32, (8, LANES), 1)
                    edge_ref[base + at : base + at + 8, :] = jnp.where(lane < 64, a, pltpu.roll(b, 64, 1))


def transport(neighbours, level, cells_ref, own_ref, a_ref, b_ref, change_ref, finish):
    me = lax.axis_index("space")
    partner = me + 1 - 2 * lax.rem(me, 2)
    ratio = COURANT * lax.shift_left(jnp.int32(1), level).astype(f32)

    def face_layers(face, base, half, shift):
        source = neighbours[0, face]
        from_own = source == me
        from_a = source == partner
        from_b = jnp.logical_and(source >= 0, jnp.logical_not(jnp.logical_or(from_own, from_a)))
        layers = []
        for layer in range(5):
            at = slice(base + layer * BSIDE + 8 * half, base + layer * BSIDE + 8 * half + 8)
            value = jnp.where(from_b, b_ref[at, :], 0.0)
            value = jnp.where(from_a, a_ref[at, :], value)
            value = jnp.where(from_own, own_ref[at, :], value)
            layers.append(pltpu.roll(value, 64, 1) if shift else value)
        return layers

    for tile in range(TILES):
        last = tile == TILES - 1
        first, second = velocity_lanes(tile)
        base = tile * 2 * EDGE
        for half in range(2):
            at = base if last else base + EDGE
            cells = [cells_ref[tile, column_place(j, half), :] for j in range(BSIDE)]
            lower = face_layers(2, at, half, last)
            upper = face_layers(3, at, half, last)
            change = along(cells, lower, upper, second < 0, jnp.abs(second))
            for j in range(BSIDE):
                change_ref[tile, column_place(j, half), :] = change[j]
        for half in range(2):
            cells = [row_cells(cells_ref, tile, i, half) for i in range(BSIDE)]
            lower = face_layers(0, base, half, False)
            upper = face_layers(1, base, half, False)
            change = along(cells, lower, upper, first < 0, jnp.abs(first))
            for i in range(BSIDE):
                total = row_cells(change_ref, tile, i, half) + change[i]
                finish(tile, i, half, cells[i], ratio * total)


def pack_kernel(x_ref, cells_ref, edge_ref):
    for tile in range(TILES - 1):
        cells_ref[tile] = x_ref[0, :, tile * LANES : (tile + 1) * LANES]
    cells_ref[TILES - 1] = jnp.zeros((CELLS, LANES), f32)
    cells_ref[TILES - 1, :, :TAIL] = x_ref[0, :, (TILES - 1) * LANES :]
    write_edges(cells_ref, edge_ref)


def first_kernel(near_ref, level_ref, x_ref, own_ref, a_ref, b_ref, out_ref, edge_ref, change_ref):
    def finish(tile, i, half, old, change):
        out_ref[tile, i * BSIDE + 8 * half : i * BSIDE + 8 * half + 8, :] = old - change

    transport(near_ref, level_ref[0], x_ref, own_ref, a_ref, b_ref, change_ref, finish)
    write_edges(out_ref, edge_ref)


def slots(mask_ref):
    marked = mask_ref[...].astype(f32)
    below = lax.broadcasted_iota(jnp.int32, (CELLS, CELLS), 0) <= lax.broadcasted_iota(jnp.int32, (CELLS, CELLS), 1)
    rank = dot(jnp.broadcast_to(marked, (8, CELLS)).astype(bf16), below.astype(f32).astype(bf16))[:1]
    slot = lax.broadcasted_iota(jnp.int32, (ACT, CELLS), 0).astype(f32) + 1.0
    hit = jnp.logical_and(slot == rank, marked > 0.5)
    return hit.astype(f32).astype(bf16)


def second_kernel(near_ref, level_ref, mask_ref, base_ref, x_ref, own_ref, a_ref, b_ref, out_ref, send_ref, change_ref):
    def finish(tile, i, half, old, change):
        start = row_cells(base_ref, tile, i, half)
        out_ref[tile, i * BSIDE + 8 * half : i * BSIDE + 8 * half + 8, :] = 0.5 * start + 0.5 * (old - change)

    transport(near_ref, level_ref[0], x_ref, own_ref, a_ref, b_ref, change_ref, finish)
    pick = slots(mask_ref)
    for pair in range(2):
        cells = jnp.concatenate([out_ref[2 * pair], out_ref[2 * pair + 1]], axis=1)
        high, low = split(cells)
        picked = dot(pick, high) + dot(pick, low)
        for side in range(2):
            for c in range(OWN):
                send_ref[pl.ds((2 * pair + side) * OWN + c, GROUP, stride=CHUNK), :] = picked[
                    c * GROUP : (c + 1) * GROUP, side * LANES : (side + 1) * LANES
                ]


def last_kernel(mask_ref, cells_ref, got_ref, out_ref):
    pick = slots(mask_ref)
    for pair in range(2):
        got = jnp.concatenate(
            [
                jnp.concatenate(
                    [got_ref[pl.ds(tile * OWN + c, GROUP, stride=CHUNK), :] for c in range(OWN)], axis=0
                )
                for tile in (2 * pair, 2 * pair + 1)
            ],
            axis=1,
        )
        high, low = split(got)
        put = lambda piece: lax.dot_general(pick, piece, (((0,), (0,)), ((), ())), preferred_element_type=f32)
        change = put(high) + put(low)
        for side in range(2):
            tile = 2 * pair + side
            wide = TAIL if tile == TILES - 1 else LANES
            out_ref[0, :, tile * LANES : tile * LANES + wide] = (
                cells_ref[tile] + change[:, side * LANES : (side + 1) * LANES]
            )[:, :wide]


def collide_kernel(
    got_ref, first_ref, second_ref, loss_ref, ph_ref, pl_ref, fh_ref, fl_ref, bh_ref, bl_ref, out_ref, x_ref, gain_ref
):
    rows = OWN * VDIM
    for c in range(OWN):
        part = []
        for m in range(4):
            tiles = [got_ref[pl.ds(m * CHUNK + t * OWN + c, 8, stride=4 * CHUNK), :] for t in range(TILES)]
            part.append(jnp.concatenate([*tiles[:3], tiles[3][:, :TAIL]], axis=1))
        x_ref[c * VDIM : c * VDIM + 8, :] = jnp.concatenate([part[0], part[1][:, :144]], axis=1)
        x_ref[c * VDIM + 8 : c * VDIM + 16, :] = jnp.concatenate([part[1][:, 144:], part[2][:, :288]], axis=1)
        x_ref[c * VDIM + 16 : c * VDIM + 24, :] = jnp.concatenate([part[2][:, 288:], part[3]], axis=1)
    plane = (ph_ref[...], pl_ref[...])
    spectrum = product(split(x_ref[...]), plane)
    spectrum = product((fh_ref[...], fl_ref[...]), split(spectrum))

    def weighted(table):
        return jnp.concatenate([spectrum[c * VDIM : (c + 1) * VDIM] * table for c in range(OWN)], axis=0)

    back = (bh_ref[...], bl_ref[...])
    gain_ref[...] = jnp.zeros_like(gain_ref)
    for t in range(TERMS):
        scaled = jnp.concatenate([weighted(first_ref[t]), weighted(second_ref[t])], axis=0)
        image = product(back, split(product(split(scaled), plane)))
        gain_ref[...] += image[:rows] * image[rows:]
    image = product(
        (bh_ref[:rows, :rows], bl_ref[:rows, :rows]), split(product(split(weighted(loss_ref[...])), plane))
    )
    gain_ref[...] = gain_ref[...] - x_ref[...] * image
    for c in range(OWN):
        r0 = gain_ref[c * VDIM : c * VDIM + 8, :]
        r1 = gain_ref[c * VDIM + 8 : c * VDIM + 16, :]
        r2 = gain_ref[c * VDIM + 16 : c * VDIM + 24, :]
        part = [
            r0[:, :WIDTH],
            jnp.concatenate([r0[:, WIDTH:], r1[:, :288]], axis=1),
            jnp.concatenate([r1[:, 288:], r2[:, :144]], axis=1),
            r2[:, 144:],
        ]
        blank = jnp.zeros((8, LANES - TAIL), f32)
        for m in range(4):
            for t in range(TILES):
                piece = part[m][:, t * LANES : min((t + 1) * LANES, WIDTH)]
                if t == TILES - 1:
                    piece = jnp.concatenate([piece, blank], axis=1)
                out_ref[pl.ds(m * CHUNK + t * OWN + c, 8, stride=4 * CHUNK), :] = piece


SMALL = pl.BlockSpec(memory_space=pltpu.SMEM)
BIG = pl.BlockSpec(memory_space=pltpu.VMEM)
PARAMS = pltpu.CompilerParams(vmem_limit_bytes=48 * 1024 * 1024)


def shape(*dims):
    return jax.ShapeDtypeStruct(dims, f32)


def call(kernel, small, big, outs, scratch=(), name=None):
    return pl.pallas_call(
        kernel,
        out_shape=outs,
        in_specs=[SMALL] * len(small) + [BIG] * len(big),
        out_specs=jax.tree.map(lambda _: BIG, outs),
        scratch_shapes=list(scratch),
        compiler_params=PARAMS,
        name=name,
    )(*small, *big)


def swap_edges(edge):
    count = lax.axis_size("space")
    pair = [(i, i ^ 1) for i in range(count)]
    other = [(i, (((i + 1) ^ 1) - 1) % count) for i in range(count)]
    return lax.ppermute(edge, "space", pair), lax.ppermute(edge, "space", other)


def shards(
    distribution, neighbours, block_level, collide_mask, gain_first, gain_second, loss_rates
):
    pieces = hartley_pieces()
    tiles = shape(TILES, CELLS, LANES)
    edges = shape(7 * EDGE, LANES)
    packed = shape(GROUP * CHUNK, LANES)
    change = pltpu.VMEM((TILES, CELLS, LANES), f32)
    mask = collide_mask.reshape(1, CELLS)

    cells, edge = call(pack_kernel, [], [distribution], (tiles, edges), name="pack_edges")
    near_a, near_b = swap_edges(edge)
    one, edge_one = call(
        first_kernel,
        [neighbours, block_level],
        [cells, edge, near_a, near_b],
        (tiles, edges),
        [change],
        name="first_section",
    )
    near_a, near_b = swap_edges(edge_one)
    two, send = call(
        second_kernel,
        [neighbours, block_level],
        [mask, cells, one, edge_one, near_a, near_b],
        (tiles, packed),
        [change],
        name="second_section",
    )
    got = lax.all_to_all(send, "vel", split_axis=0, concat_axis=0, tiled=True)
    collided = call(
        collide_kernel,
        [],
        [
            got,
            gain_first.reshape(TERMS, VDIM, PLANE),
            gain_second.reshape(TERMS, VDIM, PLANE),
            loss_rates.reshape(VDIM, PLANE),
            *pieces,
        ],
        packed,
        [pltpu.VMEM((OWN * VDIM, PLANE), f32)] * 2,
        name="collide",
    )
    back = lax.all_to_all(collided, "vel", split_axis=0, concat_axis=0, tiled=True)
    return call(
        last_kernel, [], [mask, two, back], shape(1, CELLS, WIDTH), name="add_collision"
    )


def solution(mesh):
    in_specs = (P("space", None, "vel"), P("space", None), P("space"), P("space"), P(), P(), P())
    out_specs = P("space", None, "vel")
    return jax.shard_map(shards, mesh=mesh, in_specs=in_specs, out_specs=out_specs, check_vma=False)
```

```python
import jax
import jax.numpy as jnp
import ml_dtypes
import numpy as np
from jax import lax
from jax.experimental import pallas as pl
from jax.experimental.pallas import tpu as pltpu
from jax.sharding import PartitionSpec as P

BSIDE = 16
VDIM = 24
CELLS = BSIDE * BSIDE
TERMS = 6
ACT = 128
LANES = 128
WIDTH = 432
TILES = 4
TAIL = WIDTH - 3 * LANES
GROUP = 32
OWN = ACT // GROUP
CHUNK = TILES * OWN
PLANE = VDIM * VDIM
EDGE = 5 * BSIDE
COURANT = 0.2
EPS = 1e-06

f32 = jnp.float32
bf16 = jnp.bfloat16


HALF = VDIM // 2
QUARTER = HALF * HALF
WIDE = 5 * LANES


def quarter_lane(quarter, place):
    return np.where(place < LANES, quarter * LANES + place, 4 * LANES + quarter * 16 + place - LANES)


def hartley_pieces():
    k = np.arange(VDIM)
    angle = 2.0 * np.pi * ((k[:, None] * k[None, :]) % VDIM) / VDIM
    table = (np.cos(angle) + np.sin(angle)) / np.sqrt(VDIM)
    place = np.arange(VDIM)
    first = 3 * (place % 8) + place // 8

    def pieces(array):
        high = array.astype(ml_dtypes.bfloat16)
        low = (array - high.astype(np.float64)).astype(ml_dtypes.bfloat16)
        return jnp.asarray(high), jnp.asarray(low)

    j, c = np.divmod(np.arange(PLANE), VDIM)
    physical = np.zeros((PLANE, WIDE))
    physical[
        np.arange(PLANE), quarter_lane(2 * (j // HALF) + c // HALF, (j % HALF) * HALF + c % HALF)
    ] = 1.0
    spectral = np.zeros((PLANE, WIDE))
    spectral[np.arange(PLANE), quarter_lane(2 * (j % 2) + c % 2, (j // 2) * HALF + c // 2)] = 1.0

    blocks = np.zeros((4, 2 * LANES, 2 * LANES))
    spot = np.arange(QUARTER)
    for q in range(4):
        jp, kp = divmod(q, 2)
        block = np.kron(table[:HALF, jp::2], table[:HALF, kp::2])
        column = np.where(spot < LANES, spot, LANES + 16 * q + spot - LANES)
        blocks[q][np.ix_(np.arange(LANES), column)] = block[:LANES]
        for g in range(4):
            jh, kh = divmod(g, 2)
            row = LANES + 16 * g + np.arange(QUARTER - LANES)
            blocks[q][np.ix_(row, column)] = (-1.0) ** (jh * jp + kh * kp) * block[LANES:]
    forward = np.kron(np.eye(OWN), table[:, first])
    back = np.kron(np.eye(2 * OWN), table[first, :])
    return dict(
        place=jnp.asarray(physical.astype(ml_dtypes.bfloat16)),
        unplace=jnp.asarray(physical.T.astype(ml_dtypes.bfloat16)),
        order=jnp.asarray(spectral.astype(ml_dtypes.bfloat16)),
        plane_forward=pieces(blocks),
        plane_back=pieces(blocks.transpose(0, 2, 1)),
        row_forward=pieces(forward),
        row_back=pieces(back),
    )


def dot(a, b):
    return jnp.dot(a, b, preferred_element_type=f32)


def split(a):
    high = a.astype(bf16)
    return high, (a - high.astype(f32)).astype(bf16)


def product(a, b):
    return dot(a[0], b[0]) + dot(a[1], b[0]) + dot(a[0], b[1])


def velocity_lanes(tile):
    start = lax.axis_index("vel") * WIDTH + tile * LANES
    lane = lax.broadcasted_iota(jnp.int32, (8, LANES), 1)
    g = (start + lane).astype(f32)
    rows = jnp.floor((g + 0.5) * (1.0 / VDIM))
    first = jnp.floor((rows + 0.5) * (1.0 / VDIM))
    second = rows - VDIM * first
    half = (VDIM - 1) / 2.0
    return (first - half) / half, (second - half) / half


def interface_values(u):
    count = len(u) - 4
    d = [u[m + 1] - u[m] for m in range(count + 3)]
    twice = [a + a for a in d]
    low, mid, high, rise, fall, side = {}, {}, {}, {}, {}, {}
    for m in range(count + 2):
        left, right = d[m], d[m + 1]
        bend = right - left
        base = bend * bend * (13.0 / 3.0) + 4.0 * EPS
        if m < count:
            rise[m] = twice[m + 1] + bend
            t = base + rise[m] * rise[m]
            low[m] = t * t
        if 1 <= m <= count:
            side[m] = left + right
            t = base + side[m] * side[m]
            mid[m] = t * t
        if m >= 2:
            fall[m] = bend - twice[m]
            t = base + fall[m] * fall[m]
            high[m] = t * t
    values = []
    for i in range(count):
        s0, s1, s2 = low[i], mid[i + 1], high[i + 2]
        d1, d2 = d[i + 1], d[i + 2]
        w0 = s1 * s2 * (1.0 / 3.0)
        w1 = s0 * s2 * 2.0
        w2 = s0 * s1
        p0 = rise[i] + rise[i] - d1
        p1 = side[i + 1] + d2
        p2 = d2 - fall[i + 2]
        top = w0 * p0 + w1 * p1 + w2 * p2
        values.append(u[i + 2] + top / (6.0 * (w0 + w1 + w2)))
    return values


def inner_steps(cells, neg):
    wind = [jnp.where(neg, cells[BSIDE - 1 - i], cells[i]) for i in range(BSIDE)]
    values = interface_values(wind)
    return {
        0: values[0],
        BSIDE - 1: values[-1],
        **{i: values[i - 2] - values[i - 3] for i in range(3, BSIDE - 2)},
    }


def finished_steps(inner, cells, lower, upper, neg, speed):
    n = BSIDE
    wind = {i: jnp.where(neg, cells[n - 1 - i], cells[i]) for i in (0, 1, 2, 3, n - 4, n - 3, n - 2, n - 1)}
    start = interface_values(
        [
            jnp.where(neg, upper[4], lower[4]),
            jnp.where(neg, upper[1], lower[2]),
            jnp.where(neg, upper[0], lower[3]),
            *[wind[i] for i in range(4)],
        ]
    )
    end = interface_values(
        [
            *[wind[i] for i in range(n - 4, n)],
            jnp.where(neg, lower[3], upper[0]),
            jnp.where(neg, lower[2], upper[1]),
        ]
    )
    steps = [
        start[1] - start[0],
        start[2] - start[1],
        inner[0] - start[2],
        *[inner[i] for i in range(3, n - 2)],
        end[0] - inner[n - 1],
        end[1] - end[0],
    ]
    steps = [speed * s for s in steps]
    return [jnp.where(neg, steps[n - 1 - i], steps[i]) for i in range(n)]


def row_cells(ref, tile, i, half):
    return ref[tile, i * BSIDE + 8 * half : i * BSIDE + 8 * half + 8, :]


def column_place(j, half):
    return pl.ds(8 * half * BSIDE + j, 8, stride=BSIDE)


def write_edges(cells_ref, edge_ref):
    for tile in range(TILES):
        first, second = velocity_lanes(tile)
        for half in range(2):
            for layer, i in enumerate((0, 1, 14, 15, None)):
                if i is None:
                    a = jnp.where(first < 0, row_cells(cells_ref, tile, 2, half), row_cells(cells_ref, tile, 13, half))
                    b = jnp.where(
                        second < 0,
                        cells_ref[tile, column_place(2, half), :],
                        cells_ref[tile, column_place(13, half), :],
                    )
                else:
                    a = row_cells(cells_ref, tile, i, half)
                    b = cells_ref[tile, column_place(i, half), :]
                at = layer * BSIDE + 8 * half
                if tile < TILES - 1:
                    base = tile * 2 * EDGE
                    edge_ref[base + at : base + at + 8, :] = a
                    edge_ref[base + EDGE + at : base + EDGE + at + 8, :] = b
                else:
                    base = tile * 2 * EDGE
                    lane = lax.broadcasted_iota(jnp.int32, (8, LANES), 1)
                    edge_ref[base + at : base + at + 8, :] = jnp.where(lane < 64, a, pltpu.roll(b, 64, 1))


def inner_kernel(cells_ref, inner_ref):
    for tile in range(TILES):
        first, second = velocity_lanes(tile)
        for half in range(2):
            rows = slice(8 * half, 8 * half + 8)
            cells = [cells_ref[tile, column_place(j, half), :] for j in range(BSIDE)]
            for slot, value in inner_steps(cells, second < 0).items():
                inner_ref[1, tile, slot, rows, :] = value
            cells = [row_cells(cells_ref, tile, i, half) for i in range(BSIDE)]
            for slot, value in inner_steps(cells, first < 0).items():
                inner_ref[0, tile, slot, rows, :] = value


SLOTS = (0, *range(3, BSIDE - 2), BSIDE - 1)


def transport(neighbours, level, cells_ref, inner_ref, own_ref, a_ref, b_ref, change_ref, finish):
    me = lax.axis_index("space")
    partner = me + 1 - 2 * lax.rem(me, 2)
    ratio = COURANT * lax.shift_left(jnp.int32(1), level).astype(f32)

    def face_layers(face, base, half, shift):
        source = neighbours[0, face]
        from_own = source == me
        from_a = source == partner
        from_b = jnp.logical_and(source >= 0, jnp.logical_not(jnp.logical_or(from_own, from_a)))
        layers = []
        for layer in range(5):
            at = slice(base + layer * BSIDE + 8 * half, base + layer * BSIDE + 8 * half + 8)
            value = jnp.where(from_b, b_ref[at, :], 0.0)
            value = jnp.where(from_a, a_ref[at, :], value)
            value = jnp.where(from_own, own_ref[at, :], value)
            layers.append(pltpu.roll(value, 64, 1) if shift else value)
        return layers

    for tile in range(TILES):
        last = tile == TILES - 1
        first, second = velocity_lanes(tile)
        base = tile * 2 * EDGE
        for half in range(2):
            at = base if last else base + EDGE
            cells = [cells_ref[tile, column_place(j, half), :] for j in range(BSIDE)]
            lower = face_layers(2, at, half, last)
            upper = face_layers(3, at, half, last)
            inner = {slot: inner_ref[1, tile, slot, 8 * half : 8 * half + 8, :] for slot in SLOTS}
            change = finished_steps(inner, cells, lower, upper, second < 0, jnp.abs(second))
            for j in range(BSIDE):
                change_ref[tile, column_place(j, half), :] = change[j]
        for half in range(2):
            cells = [row_cells(cells_ref, tile, i, half) for i in range(BSIDE)]
            lower = face_layers(0, base, half, False)
            upper = face_layers(1, base, half, False)
            inner = {slot: inner_ref[0, tile, slot, 8 * half : 8 * half + 8, :] for slot in SLOTS}
            change = finished_steps(inner, cells, lower, upper, first < 0, jnp.abs(first))
            for i in range(BSIDE):
                total = row_cells(change_ref, tile, i, half) + change[i]
                finish(tile, i, half, cells[i], ratio * total)


def pack_kernel(x_ref, cells_ref, edge_ref):
    for tile in range(TILES):
        piece = x_ref[0, tile * LANES : min((tile + 1) * LANES, WIDTH), :]
        if tile == TILES - 1:
            piece = jnp.concatenate([piece, jnp.zeros((LANES - TAIL, CELLS), f32)], axis=0)
        cells_ref[tile] = piece.T
    write_edges(cells_ref, edge_ref)


def first_kernel(near_ref, level_ref, x_ref, inner_ref, own_ref, a_ref, b_ref, out_ref, edge_ref, change_ref):
    def finish(tile, i, half, old, change):
        out_ref[tile, i * BSIDE + 8 * half : i * BSIDE + 8 * half + 8, :] = old - change

    transport(near_ref, level_ref[0], x_ref, inner_ref, own_ref, a_ref, b_ref, change_ref, finish)
    write_edges(out_ref, edge_ref)


def slots(mask_ref):
    marked = mask_ref[...].astype(f32)
    below = lax.broadcasted_iota(jnp.int32, (CELLS, CELLS), 0) <= lax.broadcasted_iota(jnp.int32, (CELLS, CELLS), 1)
    rank = dot(jnp.broadcast_to(marked, (8, CELLS)).astype(bf16), below.astype(f32).astype(bf16))[:1]
    slot = lax.broadcasted_iota(jnp.int32, (ACT, CELLS), 0).astype(f32) + 1.0
    hit = jnp.logical_and(slot == rank, marked > 0.5)
    return hit.astype(f32).astype(bf16)


def inner_slots_kernel(mask_ref, cells_ref, inner_ref, pick_ref):
    inner_kernel(cells_ref, inner_ref)
    pick_ref[...] = slots(mask_ref)


def second_kernel(
    near_ref, level_ref, pick_ref, base_ref, x_ref, inner_ref, own_ref, a_ref, b_ref, out_ref, send_ref, change_ref
):
    def finish(tile, i, half, old, change):
        start = row_cells(base_ref, tile, i, half)
        out_ref[tile, i * BSIDE + 8 * half : i * BSIDE + 8 * half + 8, :] = 0.5 * start + 0.5 * (old - change)

    transport(near_ref, level_ref[0], x_ref, inner_ref, own_ref, a_ref, b_ref, change_ref, finish)
    pick = pick_ref[...]
    for pair in range(2):
        cells = jnp.concatenate([out_ref[2 * pair], out_ref[2 * pair + 1]], axis=1)
        high, low = split(cells)
        picked = dot(pick, high) + dot(pick, low)
        for side in range(2):
            for c in range(OWN):
                send_ref[pl.ds((2 * pair + side) * OWN + c, GROUP, stride=CHUNK), :] = picked[
                    c * GROUP : (c + 1) * GROUP, side * LANES : (side + 1) * LANES
                ]


def last_kernel(pick_ref, cells_ref, got_ref, out_ref):
    pick = pick_ref[...]
    for pair in range(2):
        got = jnp.concatenate(
            [
                jnp.concatenate(
                    [got_ref[pl.ds(tile * OWN + c, GROUP, stride=CHUNK), :] for c in range(OWN)], axis=0
                )
                for tile in (2 * pair, 2 * pair + 1)
            ],
            axis=1,
        )
        high, low = split(got)
        put = lambda piece: lax.dot_general(pick, piece, (((0,), (0,)), ((), ())), preferred_element_type=f32)
        change = put(high) + put(low)
        for side in range(2):
            tile = 2 * pair + side
            wide = TAIL if tile == TILES - 1 else LANES
            total = cells_ref[tile] + change[:, side * LANES : (side + 1) * LANES]
            out_ref[0, tile * LANES : tile * LANES + wide, :] = total.T[:wide]


def order_kernel(first_ref, second_ref, loss_ref, order_ref, first_out, second_out, loss_out):
    order = order_ref[...]
    for table, out in ((first_ref, first_out), (second_ref, second_out), (loss_ref, loss_out)):
        high, low = split(table[...])
        out[...] = dot(high, order) + dot(low, order)


def quarters(wide):
    return [wide[:, q * LANES : (q + 1) * LANES] for q in range(5)]


def mixed(mains):
    a, b, c, d = mains
    e, f, g, h = a + b, a - b, c + d, c - d
    return [e + g, f + h, e - g, f - h]


def plane_product(tiles, high_ref, low_ref):
    parts = [split(t) for t in tiles]
    mains, shared = [], None
    for q in range(4):
        high = jnp.concatenate([parts[q][0], parts[4][0]], axis=1)
        low = jnp.concatenate([parts[q][1], parts[4][1]], axis=1)
        both = product((high, low), (high_ref[q], low_ref[q]))
        mains.append(both[:, :LANES])
        shared = both[:, LANES:] if shared is None else shared + both[:, LANES:]
    return [*mains, shared]


def row_product(table, tiles):
    return quarters(product(table, split(jnp.concatenate(tiles, axis=1))))


def collide_kernel(
    got_ref,
    first_ref,
    second_ref,
    loss_ref,
    place_ref,
    unplace_ref,
    gh_ref,
    gl_ref,
    ih_ref,
    il_ref,
    fh_ref,
    fl_ref,
    bh_ref,
    bl_ref,
    out_ref,
    x_ref,
    gain_ref,
):
    rows = OWN * VDIM
    for c in range(OWN):
        part = []
        for m in range(4):
            tiles = [got_ref[pl.ds(m * CHUNK + t * OWN + c, 8, stride=4 * CHUNK), :] for t in range(TILES)]
            part.append(jnp.concatenate([*tiles[:3], tiles[3][:, :TAIL]], axis=1))
        x_ref[c * VDIM : c * VDIM + 8, :PLANE] = jnp.concatenate([part[0], part[1][:, :144]], axis=1)
        x_ref[c * VDIM + 8 : c * VDIM + 16, :PLANE] = jnp.concatenate([part[1][:, 144:], part[2][:, :288]], axis=1)
        x_ref[c * VDIM + 16 : c * VDIM + 24, :PLANE] = jnp.concatenate([part[2][:, 288:], part[3]], axis=1)
    high, low = split(x_ref[:, :PLANE])
    x_ref[...] = dot(high, place_ref[...]) + dot(low, place_ref[...])
    tiles = quarters(x_ref[...])
    spectrum = plane_product([*mixed(tiles[:4]), tiles[4]], gh_ref, gl_ref)
    spectrum = row_product((fh_ref[...], fl_ref[...]), spectrum)

    def weighted(tables):
        return [
            jnp.concatenate(
                [
                    spectrum[q][c * VDIM : (c + 1) * VDIM] * table[:, q * LANES : (q + 1) * LANES]
                    for table in tables
                    for c in range(OWN)
                ],
                axis=0,
            )
            for q in range(5)
        ]

    def image(tables, count):
        tiles = plane_product(weighted(tables), ih_ref, il_ref)
        tiles = row_product((bh_ref[:count, :count], bl_ref[:count, :count]), tiles)
        return [*mixed(tiles[:4]), tiles[4]]

    for t in range(TERMS):
        both = image((first_ref[t], second_ref[t]), 2 * rows)
        for q in range(5):
            term = both[q][:rows] * both[q][rows:]
            at = slice(q * LANES, (q + 1) * LANES)
            gain_ref[:, at] = term if t == 0 else gain_ref[:, at] + term
    lost = image((loss_ref[...],), rows)
    high, low = split(gain_ref[...] - x_ref[...] * jnp.concatenate(lost, axis=1))
    gain_ref[:, :PLANE] = dot(high, unplace_ref[...]) + dot(low, unplace_ref[...])
    for c in range(OWN):
        r0 = gain_ref[c * VDIM : c * VDIM + 8, :PLANE]
        r1 = gain_ref[c * VDIM + 8 : c * VDIM + 16, :PLANE]
        r2 = gain_ref[c * VDIM + 16 : c * VDIM + 24, :PLANE]
        part = [
            r0[:, :WIDTH],
            jnp.concatenate([r0[:, WIDTH:], r1[:, :288]], axis=1),
            jnp.concatenate([r1[:, 288:], r2[:, :144]], axis=1),
            r2[:, 144:],
        ]
        blank = jnp.zeros((8, LANES - TAIL), f32)
        for m in range(4):
            for t in range(TILES):
                piece = part[m][:, t * LANES : min((t + 1) * LANES, WIDTH)]
                if t == TILES - 1:
                    piece = jnp.concatenate([piece, blank], axis=1)
                out_ref[pl.ds(m * CHUNK + t * OWN + c, 8, stride=4 * CHUNK), :] = piece


SMALL = pl.BlockSpec(memory_space=pltpu.SMEM)
BIG = pl.BlockSpec(memory_space=pltpu.VMEM)
PARAMS = pltpu.CompilerParams(vmem_limit_bytes=48 * 1024 * 1024)


def shape(*dims):
    return jax.ShapeDtypeStruct(dims, f32)


def call(kernel, small, big, outs, scratch=(), name=None):
    return pl.pallas_call(
        kernel,
        out_shape=outs,
        in_specs=[SMALL] * len(small) + [BIG] * len(big),
        out_specs=jax.tree.map(lambda _: BIG, outs),
        scratch_shapes=list(scratch),
        compiler_params=PARAMS,
        name=name,
    )(*small, *big)


def swap_edges(edge):
    count = lax.axis_size("space")
    pair = [(i, i ^ 1) for i in range(count)]
    other = [(i, (((i + 1) ^ 1) - 1) % count) for i in range(count)]
    return lax.ppermute(edge, "space", pair), lax.ppermute(edge, "space", other)


def shards(
    distribution, neighbours, block_level, collide_mask, gain_first, gain_second, loss_rates
):
    pieces = hartley_pieces()
    tiles = shape(TILES, CELLS, LANES)
    edges = shape(7 * EDGE, LANES)
    packed = shape(GROUP * CHUNK, LANES)
    change = pltpu.VMEM((TILES, CELLS, LANES), f32)
    inner = shape(2, TILES, BSIDE, BSIDE, LANES)
    pick = jax.ShapeDtypeStruct((ACT, CELLS), bf16)
    mask = collide_mask.reshape(1, CELLS)
    scalars = [neighbours, block_level]

    cells, edge = call(pack_kernel, [], [distribution.swapaxes(1, 2)], (tiles, edges), name="pack_edges")
    near = swap_edges(edge)
    inside = call(inner_kernel, [], [cells], inner, name="first_inner")
    one, edge_one = call(
        first_kernel, scalars, [cells, inside, edge, *near], (tiles, edges), [change], name="first_section"
    )
    near = swap_edges(edge_one)
    inside, pick = call(inner_slots_kernel, [], [mask, one], (inner, pick), name="second_inner")
    weights = [
        gain_first.reshape(TERMS * VDIM, PLANE),
        gain_second.reshape(TERMS * VDIM, PLANE),
        loss_rates.reshape(VDIM, PLANE),
    ]
    tables = call(
        order_kernel,
        [],
        [*weights, pieces["order"]],
        tuple(shape(w.shape[0], WIDE) for w in weights),
        name="order_weights",
    )
    tables = (*(t.reshape(TERMS, VDIM, WIDE) for t in tables[:2]), tables[2])
    pick, tables = lax.optimization_barrier((pick, tables))
    two, send = call(
        second_kernel,
        scalars,
        [pick, cells, one, inside, edge_one, *near],
        (tiles, packed),
        [change],
        name="second_section",
    )
    got = lax.all_to_all(send, "vel", split_axis=0, concat_axis=0, tiled=True)
    collided = call(
        collide_kernel,
        [],
        [
            got,
            *tables,
            pieces["place"],
            pieces["unplace"],
            *pieces["plane_forward"],
            *pieces["plane_back"],
            *pieces["row_forward"],
            *pieces["row_back"],
        ],
        packed,
        [pltpu.VMEM((OWN * VDIM, WIDE), f32)] * 2,
        name="collide",
    )
    back = lax.all_to_all(collided, "vel", split_axis=0, concat_axis=0, tiled=True)
    total = call(last_kernel, [], [pick, two, back], shape(1, WIDTH, CELLS), name="add_collision")
    return total.swapaxes(1, 2)


def solution(mesh):
    in_specs = (P("space", None, "vel"), P("space", None), P("space"), P("space"), P(), P(), P())
    out_specs = P("space", None, "vel")
    return jax.shard_map(shards, mesh=mesh, in_specs=in_specs, out_specs=out_specs, check_vma=False)
```

```python
import jax
import jax.numpy as jnp
import ml_dtypes
import numpy as np
from jax import lax
from jax.experimental import pallas as pl
from jax.experimental.pallas import tpu as pltpu
from jax.sharding import PartitionSpec as P

BSIDE = 16
VDIM = 24
CELLS = BSIDE * BSIDE
TERMS = 6
ACT = 128
LANES = 128
WIDTH = 432
TILES = 4
TAIL = WIDTH - 3 * LANES
GROUP = 32
OWN = ACT // GROUP
CHUNK = TILES * OWN
PLANE = VDIM * VDIM
EDGE = 5 * BSIDE
COURANT = 0.2
EPS = 1e-06

f32 = jnp.float32
bf16 = jnp.bfloat16


HALF = VDIM // 2
QUARTER = HALF * HALF
WIDE = 5 * LANES


def quarter_lane(quarter, place):
    return np.where(place < LANES, quarter * LANES + place, 4 * LANES + quarter * 16 + place - LANES)


def hartley_pieces():
    k = np.arange(VDIM)
    angle = 2.0 * np.pi * ((k[:, None] * k[None, :]) % VDIM) / VDIM
    table = (np.cos(angle) + np.sin(angle)) / np.sqrt(VDIM)

    def pieces(array):
        high = array.astype(ml_dtypes.bfloat16)
        low = (array - high.astype(np.float64)).astype(ml_dtypes.bfloat16)
        return jnp.asarray(high), jnp.asarray(low)

    j, c = np.divmod(np.arange(PLANE), VDIM)
    physical = np.zeros((PLANE, WIDE))
    physical[
        np.arange(PLANE), quarter_lane(2 * (j // HALF) + c // HALF, (j % HALF) * HALF + c % HALF)
    ] = 1.0
    spectral = np.zeros((2, WIDE, WIDE))
    for odd in range(2):
        skip = odd * (LANES // 2)
        spectral[odd, skip + np.arange(PLANE), quarter_lane(2 * (j % 2) + c % 2, (j // 2) * HALF + c // 2)] = 1.0

    blocks = np.zeros((4, 2 * LANES, 2 * LANES))
    spot = np.arange(QUARTER)
    for q in range(4):
        jp, kp = divmod(q, 2)
        block = np.kron(table[:HALF, jp::2], table[:HALF, kp::2])
        column = np.where(spot < LANES, spot, LANES + 16 * q + spot - LANES)
        blocks[q][np.ix_(np.arange(LANES), column)] = block[:LANES]
        for g in range(4):
            jh, kh = divmod(g, 2)
            row = LANES + 16 * g + np.arange(QUARTER - LANES)
            blocks[q][np.ix_(row, column)] = (-1.0) ** (jh * jp + kh * kp) * block[LANES:]
    blocks = blocks / np.sqrt(VDIM)
    return dict(
        place=jnp.asarray(physical.astype(ml_dtypes.bfloat16)),
        unplace=jnp.asarray(physical.T.astype(ml_dtypes.bfloat16)),
        order=[jnp.asarray(o.astype(ml_dtypes.bfloat16)) for o in spectral],
        plane_forward=pieces(blocks),
        plane_back=pieces(blocks.transpose(0, 2, 1)),
    )


def dot(a, b):
    return jnp.dot(a, b, preferred_element_type=f32)


def split(a):
    high = a.astype(bf16)
    return high, (a - high.astype(f32)).astype(bf16)


def product(a, b):
    return dot(a[0], b[0]) + dot(a[1], b[0]) + dot(a[0], b[1])


def velocity_lanes(tile):
    start = lax.axis_index("vel") * WIDTH + tile * LANES
    lane = lax.broadcasted_iota(jnp.int32, (8, LANES), 1)
    g = (start + lane).astype(f32)
    rows = jnp.floor((g + 0.5) * (1.0 / VDIM))
    first = jnp.floor((rows + 0.5) * (1.0 / VDIM))
    second = rows - VDIM * first
    half = (VDIM - 1) / 2.0
    return (first - half) / half, (second - half) / half


def interface_values(u):
    count = len(u) - 4
    d = [u[m + 1] - u[m] for m in range(count + 3)]
    twice = [a + a for a in d]
    low, mid, high, rise, fall, side = {}, {}, {}, {}, {}, {}
    for m in range(count + 2):
        left, right = d[m], d[m + 1]
        bend = right - left
        base = bend * bend * (13.0 / 3.0) + 4.0 * EPS
        if m < count:
            rise[m] = twice[m + 1] + bend
            t = base + rise[m] * rise[m]
            low[m] = t * t
        if 1 <= m <= count:
            side[m] = left + right
            t = base + side[m] * side[m]
            mid[m] = t * t
        if m >= 2:
            fall[m] = bend - twice[m]
            t = base + fall[m] * fall[m]
            high[m] = t * t
    values = []
    for i in range(count):
        s0, s1, s2 = low[i], mid[i + 1], high[i + 2]
        d1, d2 = d[i + 1], d[i + 2]
        w0 = s1 * s2 * (1.0 / 3.0)
        w1 = s0 * s2 * 2.0
        w2 = s0 * s1
        p0 = rise[i] + rise[i] - d1
        p1 = side[i + 1] + d2
        p2 = d2 - fall[i + 2]
        top = w0 * p0 + w1 * p1 + w2 * p2
        values.append(u[i + 2] + top / (6.0 * (w0 + w1 + w2)))
    return values


def inner_steps(cells, neg):
    wind = [jnp.where(neg, cells[BSIDE - 1 - i], cells[i]) for i in range(BSIDE)]
    values = interface_values(wind)
    return {
        0: values[0],
        BSIDE - 1: values[-1],
        **{i: values[i - 2] - values[i - 3] for i in range(3, BSIDE - 2)},
    }


def finished_steps(inner, cells, lower, upper, neg, speed):
    n = BSIDE
    wind = {i: jnp.where(neg, cells[n - 1 - i], cells[i]) for i in (0, 1, 2, 3, n - 4, n - 3, n - 2, n - 1)}
    start = interface_values(
        [
            jnp.where(neg, upper[4], lower[4]),
            jnp.where(neg, upper[1], lower[2]),
            jnp.where(neg, upper[0], lower[3]),
            *[wind[i] for i in range(4)],
        ]
    )
    end = interface_values(
        [
            *[wind[i] for i in range(n - 4, n)],
            jnp.where(neg, lower[3], upper[0]),
            jnp.where(neg, lower[2], upper[1]),
        ]
    )
    steps = [
        start[1] - start[0],
        start[2] - start[1],
        inner[0] - start[2],
        *[inner[i] for i in range(3, n - 2)],
        end[0] - inner[n - 1],
        end[1] - end[0],
    ]
    steps = [speed * s for s in steps]
    return [jnp.where(neg, steps[n - 1 - i], steps[i]) for i in range(n)]


def row_cells(ref, tile, i, half):
    return ref[tile, i * BSIDE + 8 * half : i * BSIDE + 8 * half + 8, :]


def column_place(j, half):
    return pl.ds(8 * half * BSIDE + j, 8, stride=BSIDE)


def write_edges(cells_ref, edge_ref):
    for tile in range(TILES):
        first, second = velocity_lanes(tile)
        for half in range(2):
            for layer, i in enumerate((0, 1, 14, 15, None)):
                if i is None:
                    a = jnp.where(first < 0, row_cells(cells_ref, tile, 2, half), row_cells(cells_ref, tile, 13, half))
                    b = jnp.where(
                        second < 0,
                        cells_ref[tile, column_place(2, half), :],
                        cells_ref[tile, column_place(13, half), :],
                    )
                else:
                    a = row_cells(cells_ref, tile, i, half)
                    b = cells_ref[tile, column_place(i, half), :]
                at = layer * BSIDE + 8 * half
                if tile < TILES - 1:
                    base = tile * 2 * EDGE
                    edge_ref[base + at : base + at + 8, :] = a
                    edge_ref[base + EDGE + at : base + EDGE + at + 8, :] = b
                else:
                    base = tile * 2 * EDGE
                    lane = lax.broadcasted_iota(jnp.int32, (8, LANES), 1)
                    edge_ref[base + at : base + at + 8, :] = jnp.where(lane < 64, a, pltpu.roll(b, 64, 1))


def inner_kernel(cells_ref, inner_ref):
    for tile in range(TILES):
        first, second = velocity_lanes(tile)
        for half in range(2):
            rows = slice(8 * half, 8 * half + 8)
            cells = [cells_ref[tile, column_place(j, half), :] for j in range(BSIDE)]
            for slot, value in inner_steps(cells, second < 0).items():
                inner_ref[1, tile, slot, rows, :] = value
            cells = [row_cells(cells_ref, tile, i, half) for i in range(BSIDE)]
            for slot, value in inner_steps(cells, first < 0).items():
                inner_ref[0, tile, slot, rows, :] = value


SLOTS = (0, *range(3, BSIDE - 2), BSIDE - 1)


def transport(neighbours, level, cells_ref, inner_ref, own_ref, a_ref, b_ref, change_ref, finish):
    me = lax.axis_index("space")
    partner = me + 1 - 2 * lax.rem(me, 2)
    ratio = COURANT * lax.shift_left(jnp.int32(1), level).astype(f32)

    def face_layers(face, base, half, shift):
        source = neighbours[0, face]
        from_own = source == me
        from_a = source == partner
        from_b = jnp.logical_and(source >= 0, jnp.logical_not(jnp.logical_or(from_own, from_a)))
        layers = []
        for layer in range(5):
            at = slice(base + layer * BSIDE + 8 * half, base + layer * BSIDE + 8 * half + 8)
            value = jnp.where(from_b, b_ref[at, :], 0.0)
            value = jnp.where(from_a, a_ref[at, :], value)
            value = jnp.where(from_own, own_ref[at, :], value)
            layers.append(pltpu.roll(value, 64, 1) if shift else value)
        return layers

    for tile in range(TILES):
        last = tile == TILES - 1
        first, second = velocity_lanes(tile)
        base = tile * 2 * EDGE
        for half in range(2):
            at = base if last else base + EDGE
            cells = [cells_ref[tile, column_place(j, half), :] for j in range(BSIDE)]
            lower = face_layers(2, at, half, last)
            upper = face_layers(3, at, half, last)
            inner = {slot: inner_ref[1, tile, slot, 8 * half : 8 * half + 8, :] for slot in SLOTS}
            change = finished_steps(inner, cells, lower, upper, second < 0, jnp.abs(second))
            for j in range(BSIDE):
                change_ref[tile, column_place(j, half), :] = change[j]
        for half in range(2):
            cells = [row_cells(cells_ref, tile, i, half) for i in range(BSIDE)]
            lower = face_layers(0, base, half, False)
            upper = face_layers(1, base, half, False)
            inner = {slot: inner_ref[0, tile, slot, 8 * half : 8 * half + 8, :] for slot in SLOTS}
            change = finished_steps(inner, cells, lower, upper, first < 0, jnp.abs(first))
            for i in range(BSIDE):
                total = row_cells(change_ref, tile, i, half) + change[i]
                finish(tile, i, half, cells[i], ratio * total)


def pack_kernel(x_ref, cells_ref, edge_ref):
    for tile in range(TILES):
        piece = x_ref[0, tile * LANES : min((tile + 1) * LANES, WIDTH), :]
        if tile == TILES - 1:
            piece = jnp.concatenate([piece, jnp.zeros((LANES - TAIL, CELLS), f32)], axis=0)
        cells_ref[tile] = piece.T
    write_edges(cells_ref, edge_ref)


def first_kernel(near_ref, level_ref, x_ref, inner_ref, own_ref, a_ref, b_ref, out_ref, edge_ref, change_ref):
    def finish(tile, i, half, old, change):
        out_ref[tile, i * BSIDE + 8 * half : i * BSIDE + 8 * half + 8, :] = old - change

    transport(near_ref, level_ref[0], x_ref, inner_ref, own_ref, a_ref, b_ref, change_ref, finish)
    write_edges(out_ref, edge_ref)


def slots(mask_ref):
    marked = mask_ref[...].astype(f32)
    below = lax.broadcasted_iota(jnp.int32, (CELLS, CELLS), 0) <= lax.broadcasted_iota(jnp.int32, (CELLS, CELLS), 1)
    rank = dot(jnp.broadcast_to(marked, (8, CELLS)).astype(bf16), below.astype(f32).astype(bf16))[:1]
    slot = lax.broadcasted_iota(jnp.int32, (ACT, CELLS), 0).astype(f32) + 1.0
    hit = jnp.logical_and(slot == rank, marked > 0.5)
    return hit.astype(f32).astype(bf16)


def inner_slots_kernel(mask_ref, cells_ref, inner_ref, pick_ref):
    inner_kernel(cells_ref, inner_ref)
    pick_ref[...] = slots(mask_ref)


def second_kernel(
    near_ref, level_ref, pick_ref, base_ref, x_ref, inner_ref, own_ref, a_ref, b_ref, out_ref, send_ref, change_ref
):
    def finish(tile, i, half, old, change):
        start = row_cells(base_ref, tile, i, half)
        out_ref[tile, i * BSIDE + 8 * half : i * BSIDE + 8 * half + 8, :] = 0.5 * start + 0.5 * (old - change)

    transport(near_ref, level_ref[0], x_ref, inner_ref, own_ref, a_ref, b_ref, change_ref, finish)
    pick = pick_ref[...]
    for pair in range(2):
        cells = jnp.concatenate([out_ref[2 * pair], out_ref[2 * pair + 1]], axis=1)
        high, low = split(cells)
        picked = dot(pick, high) + dot(pick, low)
        for side in range(2):
            for c in range(OWN):
                send_ref[pl.ds((2 * pair + side) * OWN + c, GROUP, stride=CHUNK), :] = picked[
                    c * GROUP : (c + 1) * GROUP, side * LANES : (side + 1) * LANES
                ]


def last_kernel(pick_ref, cells_ref, got_ref, out_ref):
    pick = pick_ref[...]
    for pair in range(2):
        got = jnp.concatenate(
            [
                jnp.concatenate(
                    [got_ref[pl.ds(tile * OWN + c, GROUP, stride=CHUNK), :] for c in range(OWN)], axis=0
                )
                for tile in (2 * pair, 2 * pair + 1)
            ],
            axis=1,
        )
        high, low = split(got)
        put = lambda piece: lax.dot_general(pick, piece, (((0,), (0,)), ((), ())), preferred_element_type=f32)
        change = put(high) + put(low)
        for side in range(2):
            tile = 2 * pair + side
            wide = TAIL if tile == TILES - 1 else LANES
            total = cells_ref[tile] + change[:, side * LANES : (side + 1) * LANES]
            out_ref[0, tile * LANES : tile * LANES + wide, :] = total.T[:wide]


def order_kernel(first_ref, second_ref, loss_ref, even_ref, odd_ref, out_one, out_two, one_ref, two_ref):
    order = (even_ref[...], odd_ref[...])
    for i in range(VDIM):
        start = i * PLANE - (i % 2) * (LANES // 2)
        window = slice(start, start + WIDE)
        at = i // 2 + (i % 2) * HALF
        one_ref[at, :TERMS, :] = first_ref[:, window]
        one_ref[at, TERMS : TERMS + 1, :] = loss_ref[:, window]
        one_ref[at, TERMS + 1 :, :] = jnp.zeros((7 - TERMS, WIDE), f32)
        two_ref[at, :TERMS, :] = second_ref[:, window]
        two_ref[at, TERMS:, :] = jnp.zeros((8 - TERMS, WIDE), f32)
    for source, out in ((one_ref, out_one), (two_ref, out_two)):
        for odd in range(2):
            high, low = split(source[odd * HALF : (odd + 1) * HALF].reshape(HALF * 8, WIDE))
            table = dot(high, order[odd]) + dot(low, order[odd])
            for m in range(HALF):
                out[2 * m + odd] = table[8 * m : 8 * m + 8]


def quarters(wide):
    return [wide[:, q * LANES : (q + 1) * LANES] for q in range(5)]


def mixed(mains):
    a, b, c, d = mains
    e, f, g, h = a + b, a - b, c + d, c - d
    return [e + g, f + h, e - g, f - h]


def plane_product(tiles, high_ref, low_ref):
    parts = [split(t) for t in tiles]
    mains, shared = [], None
    for q in range(4):
        high = jnp.concatenate([parts[q][0], parts[4][0]], axis=1)
        low = jnp.concatenate([parts[q][1], parts[4][1]], axis=1)
        both = product((high, low), (high_ref[q], low_ref[q]))
        mains.append(both[:, :LANES])
        shared = both[:, LANES:] if shared is None else shared + both[:, LANES:]
    return [*mains, shared]


COS15, COS30, COS45, COS75 = (float(np.cos(np.pi * a / 180.0)) for a in (15, 30, 45, 75))


def row_transform(x):
    e = {j: x[j] + x[24 - j] for j in range(1, 12)}
    o = {j: x[j] - x[24 - j] for j in range(1, 12)}
    c, s = {}, {}

    u = x[0] + x[12]
    a = {j: e[j] + e[12 - j] for j in range(1, 6)}
    p0, p1, p2, p3 = u + e[6], a[1] + a[5], a[2] + a[4], a[3]
    g, h, m, n = p0 + p3, p0 - p3, p1 + p2, p1 - p2
    c[0], c[4], c[8], c[12] = g + m, h + 0.5 * n, g - 0.5 * m, h - n
    q0, q1, q2 = u - e[6], COS30 * (a[1] - a[5]), a[2] - a[4]
    w = q0 + 0.5 * q2
    c[2], c[6], c[10] = w + q1, q0 - q2, w - q1
    v = x[0] - x[12]
    b = {j: e[j] - e[12 - j] for j in range(1, 6)}
    w, z = v + 0.5 * b[4], COS30 * b[2]
    even = {1: w + z, 3: v - b[4], 5: w - z}
    t = COS45 * b[3]
    odd = {
        1: COS15 * b[1] + t + COS75 * b[5],
        3: COS45 * (b[1] - b[3] - b[5]),
        5: COS75 * b[1] - t + COS15 * b[5],
    }
    for k in (1, 3, 5):
        c[k], c[12 - k] = even[k] + odd[k], even[k] - odd[k]
    a = {j: o[j] + o[12 - j] for j in range(1, 6)}
    w, z = 0.5 * a[2] + o[6], COS30 * a[4]
    even = {1: w + z, 3: a[2] - o[6], 5: w - z}
    t = COS45 * a[3]
    odd = {
        1: COS75 * a[1] + t + COS15 * a[5],
        3: COS45 * (a[1] + a[3] - a[5]),
        5: COS15 * a[1] - t + COS75 * a[5],
    }
    for k in (1, 3, 5):
        s[k], s[12 - k] = odd[k] + even[k], odd[k] - even[k]
    b = {j: o[j] - o[12 - j] for j in range(1, 6)}
    p1, p2 = b[1] + b[5], COS30 * (b[2] + b[4])
    w = 0.5 * p1 + b[3]
    s[2], s[6], s[10] = w + p2, p1 - b[3], w - p2
    p1, p2 = COS30 * (b[1] - b[5]), COS30 * (b[2] - b[4])
    s[4], s[8] = p1 + p2, p1 - p2

    out = [None] * 24
    out[0], out[12] = c[0], c[12]
    for k in range(1, 12):
        out[k], out[24 - k] = c[k] + s[k], c[k] - s[k]
    return out


def transform_rows(tiles, out_ref):
    for q in range(5):
        out = row_transform([tiles[q][8 * i : 8 * i + 8] for i in range(VDIM)])
        for i in range(VDIM):
            out_ref[q, 8 * i : 8 * i + 8, :] = out[i]


def row_image(ref, i):
    tiles = [ref[q, 8 * i : 8 * i + 8, :] for q in range(5)]
    return [*mixed(tiles[:4]), tiles[4]]


def collide_kernel(
    got_ref,
    one_ref,
    two_ref,
    place_ref,
    unplace_ref,
    gh_ref,
    gl_ref,
    ih_ref,
    il_ref,
    out_ref,
    flat_ref,
    x_ref,
    spectrum_ref,
    first_ref,
    second_ref,
    total_ref,
):
    for c in range(OWN):
        part = []
        for m in range(4):
            tiles = [got_ref[pl.ds(m * CHUNK + t * OWN + c, 8, stride=4 * CHUNK), :] for t in range(TILES)]
            part.append(jnp.concatenate([*tiles[:3], tiles[3][:, :TAIL]], axis=1))
        flat_ref[c * VDIM : c * VDIM + 8, :] = jnp.concatenate([part[0], part[1][:, :144]], axis=1)
        flat_ref[c * VDIM + 8 : c * VDIM + 16, :] = jnp.concatenate([part[1][:, 144:], part[2][:, :288]], axis=1)
        flat_ref[c * VDIM + 16 : c * VDIM + 24, :] = jnp.concatenate([part[2][:, 288:], part[3]], axis=1)
    high, low = split(flat_ref[...])
    placed = dot(high, place_ref[...]) + dot(low, place_ref[...])
    for c in range(OWN):
        for r in range(3):
            for q in range(5):
                value = placed[c * VDIM + 8 * r : c * VDIM + 8 * r + 8, q * LANES : (q + 1) * LANES]
                for copy in (0, OWN):
                    x_ref[q, pl.ds(8 * r + c + copy, 8, stride=VDIM), :] = value
    tiles = [x_ref[q] for q in range(5)]
    transform_rows(plane_product([*mixed(tiles[:4]), tiles[4]], gh_ref, gl_ref), spectrum_ref)

    upper = lax.broadcasted_iota(jnp.int32, (8, LANES), 0) < OWN

    def repeated(table_ref, i, t, q):
        return jnp.broadcast_to(table_ref[i, t : t + 1, q * LANES : (q + 1) * LANES], (8, LANES))

    def image(table_ref, top, bottom, out_ref):
        tiles = []
        for q in range(5):
            pieces = []
            for i in range(VDIM):
                table = repeated(table_ref, i, top, q)
                if bottom != top:
                    table = jnp.where(upper, table, repeated(table_ref, i, bottom, q))
                pieces.append(spectrum_ref[q, 8 * i : 8 * i + 8, :] * table)
            tiles.append(jnp.concatenate(pieces, axis=0))
        transform_rows(plane_product(tiles, ih_ref, il_ref), out_ref)

    for u in range(TERMS // 2):
        image(one_ref, 2 * u, 2 * u + 1, first_ref)
        image(two_ref, 2 * u, 2 * u + 1, second_ref)
        for i in range(VDIM):
            one, two = row_image(first_ref, i), row_image(second_ref, i)
            for q in range(5):
                at = slice(8 * i, 8 * i + 8)
                term = one[q] * two[q]
                total_ref[q, at, :] = term if u == 0 else total_ref[q, at, :] + term
    image(one_ref, TERMS, TERMS, first_ref)
    for i in range(VDIM):
        lost = row_image(first_ref, i)
        for q in range(5):
            at = slice(8 * i, 8 * i + 8)
            both = total_ref[q, at, :]
            total_ref[q, at, :] = both + pltpu.roll(both, OWN, 0) - x_ref[q, at, :] * lost[q]
    rows = [
        jnp.concatenate([total_ref[q, pl.ds(8 * r + c, 8, stride=VDIM), :] for q in range(5)], axis=1)
        for c in range(OWN)
        for r in range(3)
    ]
    high, low = split(jnp.concatenate(rows, axis=0))
    flat_ref[...] = dot(high, unplace_ref[...]) + dot(low, unplace_ref[...])
    for c in range(OWN):
        r0 = flat_ref[c * VDIM : c * VDIM + 8, :]
        r1 = flat_ref[c * VDIM + 8 : c * VDIM + 16, :]
        r2 = flat_ref[c * VDIM + 16 : c * VDIM + 24, :]
        part = [
            r0[:, :WIDTH],
            jnp.concatenate([r0[:, WIDTH:], r1[:, :288]], axis=1),
            jnp.concatenate([r1[:, 288:], r2[:, :144]], axis=1),
            r2[:, 144:],
        ]
        blank = jnp.zeros((8, LANES - TAIL), f32)
        for m in range(4):
            for t in range(TILES):
                piece = part[m][:, t * LANES : min((t + 1) * LANES, WIDTH)]
                if t == TILES - 1:
                    piece = jnp.concatenate([piece, blank], axis=1)
                out_ref[pl.ds(m * CHUNK + t * OWN + c, 8, stride=4 * CHUNK), :] = piece


SMALL = pl.BlockSpec(memory_space=pltpu.SMEM)
BIG = pl.BlockSpec(memory_space=pltpu.VMEM)
PARAMS = pltpu.CompilerParams(vmem_limit_bytes=48 * 1024 * 1024)


def shape(*dims):
    return jax.ShapeDtypeStruct(dims, f32)


def call(kernel, small, big, outs, scratch=(), name=None):
    return pl.pallas_call(
        kernel,
        out_shape=outs,
        in_specs=[SMALL] * len(small) + [BIG] * len(big),
        out_specs=jax.tree.map(lambda _: BIG, outs),
        scratch_shapes=list(scratch),
        compiler_params=PARAMS,
        name=name,
    )(*small, *big)


def swap_edges(edge):
    count = lax.axis_size("space")
    pair = [(i, i ^ 1) for i in range(count)]
    other = [(i, (((i + 1) ^ 1) - 1) % count) for i in range(count)]
    return lax.ppermute(edge, "space", pair), lax.ppermute(edge, "space", other)


def shards(
    distribution, neighbours, block_level, collide_mask, gain_first, gain_second, loss_rates
):
    pieces = hartley_pieces()
    tiles = shape(TILES, CELLS, LANES)
    edges = shape(7 * EDGE, LANES)
    packed = shape(GROUP * CHUNK, LANES)
    change = pltpu.VMEM((TILES, CELLS, LANES), f32)
    inner = shape(2, TILES, BSIDE, BSIDE, LANES)
    pick = jax.ShapeDtypeStruct((ACT, CELLS), bf16)
    mask = collide_mask.reshape(1, CELLS)
    scalars = [neighbours, block_level]
    rows = (5, VDIM * 2 * OWN, LANES)

    cells, edge = call(pack_kernel, [], [distribution.swapaxes(1, 2)], (tiles, edges), name="pack_edges")
    near = swap_edges(edge)
    inside, pick = call(inner_slots_kernel, [], [mask, cells], (inner, pick), name="first_inner")
    loss = loss_rates.reshape(1, -1)
    inside, loss = lax.optimization_barrier((inside, loss))
    one, edge_one = call(
        first_kernel, scalars, [cells, inside, edge, *near], (tiles, edges), [change], name="first_section"
    )
    near = swap_edges(edge_one)
    inside = call(inner_kernel, [], [one], inner, name="second_inner")
    table = (VDIM, 8, WIDE)
    tables = call(
        order_kernel,
        [],
        [gain_first, gain_second, loss, *pieces["order"]],
        (shape(*table), shape(*table)),
        [pltpu.VMEM(table, f32)] * 2,
        name="order_weights",
    )
    inside, tables = lax.optimization_barrier((inside, tables))
    two, send = call(
        second_kernel,
        scalars,
        [pick, cells, one, inside, edge_one, *near],
        (tiles, packed),
        [change],
        name="second_section",
    )
    got = lax.all_to_all(send, "vel", split_axis=0, concat_axis=0, tiled=True)
    collided = call(
        collide_kernel,
        [],
        [
            got,
            *tables,
            pieces["place"],
            pieces["unplace"],
            *pieces["plane_forward"],
            *pieces["plane_back"],
        ],
        packed,
        [pltpu.VMEM((OWN * VDIM, PLANE), f32)] + [pltpu.VMEM(rows, f32)] * 5,
        name="collide",
    )
    back = lax.all_to_all(collided, "vel", split_axis=0, concat_axis=0, tiled=True)
    total = call(last_kernel, [], [pick, two, back], shape(1, WIDTH, CELLS), name="add_collision")
    return total.swapaxes(1, 2)


def solution(mesh):
    in_specs = (P("space", None, "vel"), P("space", None), P("space"), P("space"), P(), P(), P())
    out_specs = P("space", None, "vel")
    return jax.shard_map(shards, mesh=mesh, in_specs=in_specs, out_specs=out_specs, check_vma=False)
```

```python
import jax
import jax.numpy as jnp
import ml_dtypes
import numpy as np
from jax import lax
from jax.experimental import pallas as pl
from jax.experimental.pallas import tpu as pltpu
from jax.sharding import PartitionSpec as P

BSIDE = 16
VDIM = 24
CELLS = BSIDE * BSIDE
TERMS = 6
ACT = 128
LANES = 128
WIDTH = 432
TILES = 4
TAIL = WIDTH - 3 * LANES
GROUP = 32
OWN = ACT // GROUP
CHUNK = TILES * OWN
PLANE = VDIM * VDIM
EDGE = 5 * BSIDE
COURANT = 0.2
EPS = 1e-06

f32 = jnp.float32
bf16 = jnp.bfloat16


HALF = VDIM // 2
QUARTER = HALF * HALF
WIDE = 5 * LANES


def quarter_lane(quarter, place):
    return np.where(place < LANES, quarter * LANES + place, 4 * LANES + quarter * 16 + place - LANES)


def hartley_pieces():
    k = np.arange(VDIM)
    angle = 2.0 * np.pi * ((k[:, None] * k[None, :]) % VDIM) / VDIM
    table = (np.cos(angle) + np.sin(angle)) / np.sqrt(VDIM)

    def pieces(array):
        high = array.astype(ml_dtypes.bfloat16)
        low = (array - high.astype(np.float64)).astype(ml_dtypes.bfloat16)
        return jnp.asarray(high), jnp.asarray(low)

    j, c = np.divmod(np.arange(PLANE), VDIM)
    physical = np.zeros((PLANE, WIDE))
    physical[
        np.arange(PLANE), quarter_lane(2 * (j // HALF) + c // HALF, (j % HALF) * HALF + c % HALF)
    ] = 1.0
    spectral = np.zeros((2, WIDE, WIDE))
    for odd in range(2):
        skip = odd * (LANES // 2)
        spectral[odd, skip + np.arange(PLANE), quarter_lane(2 * (j % 2) + c % 2, (j // 2) * HALF + c // 2)] = 1.0

    blocks = np.zeros((4, 2 * LANES, 2 * LANES))
    spot = np.arange(QUARTER)
    for q in range(4):
        jp, kp = divmod(q, 2)
        block = np.kron(table[:HALF, jp::2], table[:HALF, kp::2])
        column = np.where(spot < LANES, spot, LANES + 16 * q + spot - LANES)
        blocks[q][np.ix_(np.arange(LANES), column)] = block[:LANES]
        for g in range(4):
            jh, kh = divmod(g, 2)
            row = LANES + 16 * g + np.arange(QUARTER - LANES)
            blocks[q][np.ix_(row, column)] = (-1.0) ** (jh * jp + kh * kp) * block[LANES:]
    blocks = blocks / np.sqrt(VDIM)
    return dict(
        place=jnp.asarray(physical.astype(ml_dtypes.bfloat16)),
        unplace=jnp.asarray(physical.T.astype(ml_dtypes.bfloat16)),
        order=[jnp.asarray(o.astype(ml_dtypes.bfloat16)) for o in spectral],
        plane_forward=pieces(blocks),
        plane_back=pieces(blocks.transpose(0, 2, 1)),
    )


def dot(a, b):
    return jnp.dot(a, b, preferred_element_type=f32)


def split(a):
    high = a.astype(bf16)
    return high, (a - high.astype(f32)).astype(bf16)


def product(a, b):
    return dot(a[0], b[0]) + dot(a[1], b[0]) + dot(a[0], b[1])


def velocity_lanes(tile):
    start = lax.axis_index("vel") * WIDTH + tile * LANES
    lane = lax.broadcasted_iota(jnp.int32, (8, LANES), 1)
    g = (start + lane).astype(f32)
    rows = jnp.floor((g + 0.5) * (1.0 / VDIM))
    first = jnp.floor((rows + 0.5) * (1.0 / VDIM))
    second = rows - VDIM * first
    half = (VDIM - 1) / 2.0
    return (first - half) / half, (second - half) / half


def interface_values(u):
    count = len(u) - 4
    d = [u[m + 1] - u[m] for m in range(count + 3)]
    twice = [a + a for a in d]
    low, mid, high, rise, fall, side = {}, {}, {}, {}, {}, {}
    for m in range(count + 2):
        left, right = d[m], d[m + 1]
        bend = right - left
        base = bend * bend * (13.0 / 3.0) + 4.0 * EPS
        if m < count:
            rise[m] = twice[m + 1] + bend
            t = base + rise[m] * rise[m]
            low[m] = t * t
        if 1 <= m <= count:
            side[m] = left + right
            t = base + side[m] * side[m]
            mid[m] = t * t
        if m >= 2:
            fall[m] = bend - twice[m]
            t = base + fall[m] * fall[m]
            high[m] = t * t
    values = []
    for i in range(count):
        s0, s1, s2 = low[i], mid[i + 1], high[i + 2]
        d1, d2 = d[i + 1], d[i + 2]
        w0 = s1 * s2 * (1.0 / 3.0)
        w1 = s0 * s2 * 2.0
        w2 = s0 * s1
        p0 = rise[i] + rise[i] - d1
        p1 = side[i + 1] + d2
        p2 = d2 - fall[i + 2]
        top = w0 * p0 + w1 * p1 + w2 * p2
        values.append(u[i + 2] + top / (6.0 * (w0 + w1 + w2)))
    return values


def inner_steps(cells, neg):
    wind = [jnp.where(neg, cells[BSIDE - 1 - i], cells[i]) for i in range(BSIDE)]
    values = interface_values(wind)
    return {
        0: values[0],
        BSIDE - 1: values[-1],
        **{i: values[i - 2] - values[i - 3] for i in range(3, BSIDE - 2)},
    }


def finished_steps(inner, cells, lower, upper, neg, speed):
    n = BSIDE
    wind = {i: jnp.where(neg, cells[n - 1 - i], cells[i]) for i in (0, 1, 2, 3, n - 4, n - 3, n - 2, n - 1)}
    start = interface_values(
        [
            jnp.where(neg, upper[4], lower[4]),
            jnp.where(neg, upper[1], lower[2]),
            jnp.where(neg, upper[0], lower[3]),
            *[wind[i] for i in range(4)],
        ]
    )
    end = interface_values(
        [
            *[wind[i] for i in range(n - 4, n)],
            jnp.where(neg, lower[3], upper[0]),
            jnp.where(neg, lower[2], upper[1]),
        ]
    )
    steps = [
        start[1] - start[0],
        start[2] - start[1],
        inner[0] - start[2],
        *[inner[i] for i in range(3, n - 2)],
        end[0] - inner[n - 1],
        end[1] - end[0],
    ]
    steps = [speed * s for s in steps]
    return [jnp.where(neg, steps[n - 1 - i], steps[i]) for i in range(n)]


def row_cells(ref, tile, i, half):
    return ref[tile, i * BSIDE + 8 * half : i * BSIDE + 8 * half + 8, :]


def column_place(j, half):
    return pl.ds(8 * half * BSIDE + j, 8, stride=BSIDE)


def write_edges(cells_ref, edge_ref):
    for tile in range(TILES):
        first, second = velocity_lanes(tile)
        for half in range(2):
            for layer, i in enumerate((0, 1, 14, 15, None)):
                if i is None:
                    a = jnp.where(first < 0, row_cells(cells_ref, tile, 2, half), row_cells(cells_ref, tile, 13, half))
                    b = jnp.where(
                        second < 0,
                        cells_ref[tile, column_place(2, half), :],
                        cells_ref[tile, column_place(13, half), :],
                    )
                else:
                    a = row_cells(cells_ref, tile, i, half)
                    b = cells_ref[tile, column_place(i, half), :]
                at = layer * BSIDE + 8 * half
                if tile < TILES - 1:
                    base = tile * 2 * EDGE
                    edge_ref[base + at : base + at + 8, :] = a
                    edge_ref[base + EDGE + at : base + EDGE + at + 8, :] = b
                else:
                    base = tile * 2 * EDGE
                    lane = lax.broadcasted_iota(jnp.int32, (8, LANES), 1)
                    edge_ref[base + at : base + at + 8, :] = jnp.where(lane < 64, a, pltpu.roll(b, 64, 1))


def inner_kernel(cells_ref, inner_ref):
    for tile in range(TILES):
        first, second = velocity_lanes(tile)
        for half in range(2):
            rows = slice(8 * half, 8 * half + 8)
            cells = [cells_ref[tile, column_place(j, half), :] for j in range(BSIDE)]
            for slot, value in inner_steps(cells, second < 0).items():
                inner_ref[1, tile, slot, rows, :] = value
            cells = [row_cells(cells_ref, tile, i, half) for i in range(BSIDE)]
            for slot, value in inner_steps(cells, first < 0).items():
                inner_ref[0, tile, slot, rows, :] = value


SLOTS = (0, *range(3, BSIDE - 2), BSIDE - 1)


def transport(neighbours, level, cells_ref, inner_ref, own_ref, a_ref, b_ref, change_ref, finish):
    me = lax.axis_index("space")
    partner = me + 1 - 2 * lax.rem(me, 2)
    ratio = COURANT * lax.shift_left(jnp.int32(1), level).astype(f32)

    def face_layers(face, base, half, shift):
        source = neighbours[0, face]
        from_own = source == me
        from_a = source == partner
        from_b = jnp.logical_and(source >= 0, jnp.logical_not(jnp.logical_or(from_own, from_a)))
        layers = []
        for layer in range(5):
            at = slice(base + layer * BSIDE + 8 * half, base + layer * BSIDE + 8 * half + 8)
            value = jnp.where(from_b, b_ref[at, :], 0.0)
            value = jnp.where(from_a, a_ref[at, :], value)
            value = jnp.where(from_own, own_ref[at, :], value)
            layers.append(pltpu.roll(value, 64, 1) if shift else value)
        return layers

    for tile in range(TILES):
        last = tile == TILES - 1
        first, second = velocity_lanes(tile)
        base = tile * 2 * EDGE
        for half in range(2):
            at = base if last else base + EDGE
            cells = [cells_ref[tile, column_place(j, half), :] for j in range(BSIDE)]
            lower = face_layers(2, at, half, last)
            upper = face_layers(3, at, half, last)
            inner = {slot: inner_ref[1, tile, slot, 8 * half : 8 * half + 8, :] for slot in SLOTS}
            change = finished_steps(inner, cells, lower, upper, second < 0, jnp.abs(second))
            for j in range(BSIDE):
                change_ref[tile, column_place(j, half), :] = change[j]
        for half in range(2):
            cells = [row_cells(cells_ref, tile, i, half) for i in range(BSIDE)]
            lower = face_layers(0, base, half, False)
            upper = face_layers(1, base, half, False)
            inner = {slot: inner_ref[0, tile, slot, 8 * half : 8 * half + 8, :] for slot in SLOTS}
            change = finished_steps(inner, cells, lower, upper, first < 0, jnp.abs(first))
            for i in range(BSIDE):
                total = row_cells(change_ref, tile, i, half) + change[i]
                finish(tile, i, half, cells[i], ratio * total)


def pack_kernel(x_ref, cells_ref, edge_ref):
    for tile in range(TILES):
        piece = x_ref[0, tile * LANES : min((tile + 1) * LANES, WIDTH), :]
        if tile == TILES - 1:
            piece = jnp.concatenate([piece, jnp.zeros((LANES - TAIL, CELLS), f32)], axis=0)
        cells_ref[tile] = piece.T
    write_edges(cells_ref, edge_ref)


def first_kernel(near_ref, level_ref, x_ref, inner_ref, own_ref, a_ref, b_ref, out_ref, edge_ref, change_ref):
    def finish(tile, i, half, old, change):
        out_ref[tile, i * BSIDE + 8 * half : i * BSIDE + 8 * half + 8, :] = old - change

    transport(near_ref, level_ref[0], x_ref, inner_ref, own_ref, a_ref, b_ref, change_ref, finish)
    write_edges(out_ref, edge_ref)


def slots(mask_ref):
    marked = mask_ref[...].astype(f32)
    below = lax.broadcasted_iota(jnp.int32, (CELLS, CELLS), 0) <= lax.broadcasted_iota(jnp.int32, (CELLS, CELLS), 1)
    rank = dot(jnp.broadcast_to(marked, (8, CELLS)).astype(bf16), below.astype(f32).astype(bf16))[:1]
    slot = lax.broadcasted_iota(jnp.int32, (ACT, CELLS), 0).astype(f32) + 1.0
    hit = jnp.logical_and(slot == rank, marked > 0.5)
    return hit.astype(f32).astype(bf16)


def inner_slots_kernel(mask_ref, cells_ref, inner_ref, pick_ref):
    inner_kernel(cells_ref, inner_ref)
    pick_ref[...] = slots(mask_ref)


def second_kernel(
    near_ref, level_ref, pick_ref, base_ref, x_ref, inner_ref, own_ref, a_ref, b_ref, out_ref, send_ref, change_ref
):
    def finish(tile, i, half, old, change):
        start = row_cells(base_ref, tile, i, half)
        out_ref[tile, i * BSIDE + 8 * half : i * BSIDE + 8 * half + 8, :] = 0.5 * start + 0.5 * (old - change)

    transport(near_ref, level_ref[0], x_ref, inner_ref, own_ref, a_ref, b_ref, change_ref, finish)
    pick = pick_ref[...]
    for pair in range(2):
        cells = jnp.concatenate([out_ref[2 * pair], out_ref[2 * pair + 1]], axis=1)
        high, low = split(cells)
        picked = dot(pick, high) + dot(pick, low)
        for side in range(2):
            for c in range(OWN):
                send_ref[pl.ds((2 * pair + side) * OWN + c, GROUP, stride=CHUNK), :] = picked[
                    c * GROUP : (c + 1) * GROUP, side * LANES : (side + 1) * LANES
                ]


def last_kernel(pick_ref, cells_ref, got_ref, out_ref, total_ref, done):
    pick = pick_ref[...]
    copies = []
    for pair in range(2):
        got = jnp.concatenate(
            [
                jnp.concatenate(
                    [got_ref[pl.ds(tile * OWN + c, GROUP, stride=CHUNK), :] for c in range(OWN)], axis=0
                )
                for tile in (2 * pair, 2 * pair + 1)
            ],
            axis=1,
        )
        high, low = split(got)
        put = lambda piece: lax.dot_general(pick, piece, (((0,), (0,)), ((), ())), preferred_element_type=f32)
        change = put(high) + put(low)
        for side in range(2):
            tile = 2 * pair + side
            wide = TAIL if tile == TILES - 1 else LANES
            total = cells_ref[tile] + change[:, side * LANES : (side + 1) * LANES]
            total_ref[tile] = total.T
            copy = pltpu.make_async_copy(
                total_ref.at[tile, pl.ds(0, wide), :],
                out_ref.at[0, pl.ds(tile * LANES, wide), :],
                done.at[tile],
            )
            copy.start()
            copies.append(copy)
    for copy in copies:
        copy.wait()


def order_kernel(first_ref, second_ref, loss_ref, even_ref, odd_ref, out_one, out_two, one_ref, two_ref):
    order = (even_ref[...], odd_ref[...])
    for i in range(VDIM):
        start = i * PLANE - (i % 2) * (LANES // 2)
        window = slice(start, start + WIDE)
        at = i // 2 + (i % 2) * HALF
        one_ref[at, :TERMS, :] = first_ref[:, window]
        one_ref[at, TERMS : TERMS + 1, :] = loss_ref[:, window]
        one_ref[at, TERMS + 1 :, :] = jnp.zeros((7 - TERMS, WIDE), f32)
        two_ref[at, :TERMS, :] = second_ref[:, window]
        two_ref[at, TERMS:, :] = jnp.zeros((8 - TERMS, WIDE), f32)
    for source, out in ((one_ref, out_one), (two_ref, out_two)):
        for odd in range(2):
            high, low = split(source[odd * HALF : (odd + 1) * HALF].reshape(HALF * 8, WIDE))
            table = dot(high, order[odd]) + dot(low, order[odd])
            for m in range(HALF):
                out[2 * m + odd] = table[8 * m : 8 * m + 8]


def quarters(wide):
    return [wide[:, q * LANES : (q + 1) * LANES] for q in range(5)]


def mixed(mains):
    a, b, c, d = mains
    e, f, g, h = a + b, a - b, c + d, c - d
    return [e + g, f + h, e - g, f - h]


def plane_product(tiles, high_ref, low_ref):
    parts = [split(t) for t in tiles]
    mains, shared = [], None
    for q in range(4):
        high = jnp.concatenate([parts[q][0], parts[4][0]], axis=1)
        low = jnp.concatenate([parts[q][1], parts[4][1]], axis=1)
        both = product((high, low), (high_ref[q], low_ref[q]))
        mains.append(both[:, :LANES])
        shared = both[:, LANES:] if shared is None else shared + both[:, LANES:]
    return [*mains, shared]


COS15, COS30, COS45, COS75 = (float(np.cos(np.pi * a / 180.0)) for a in (15, 30, 45, 75))


def row_transform(x):
    e = {j: x[j] + x[24 - j] for j in range(1, 12)}
    o = {j: x[j] - x[24 - j] for j in range(1, 12)}
    c, s = {}, {}

    u = x[0] + x[12]
    a = {j: e[j] + e[12 - j] for j in range(1, 6)}
    p0, p1, p2, p3 = u + e[6], a[1] + a[5], a[2] + a[4], a[3]
    g, h, m, n = p0 + p3, p0 - p3, p1 + p2, p1 - p2
    c[0], c[4], c[8], c[12] = g + m, h + 0.5 * n, g - 0.5 * m, h - n
    q0, q1, q2 = u - e[6], COS30 * (a[1] - a[5]), a[2] - a[4]
    w = q0 + 0.5 * q2
    c[2], c[6], c[10] = w + q1, q0 - q2, w - q1
    v = x[0] - x[12]
    b = {j: e[j] - e[12 - j] for j in range(1, 6)}
    w, z = v + 0.5 * b[4], COS30 * b[2]
    even = {1: w + z, 3: v - b[4], 5: w - z}
    t = COS45 * b[3]
    odd = {
        1: COS15 * b[1] + t + COS75 * b[5],
        3: COS45 * (b[1] - b[3] - b[5]),
        5: COS75 * b[1] - t + COS15 * b[5],
    }
    for k in (1, 3, 5):
        c[k], c[12 - k] = even[k] + odd[k], even[k] - odd[k]
    a = {j: o[j] + o[12 - j] for j in range(1, 6)}
    w, z = 0.5 * a[2] + o[6], COS30 * a[4]
    even = {1: w + z, 3: a[2] - o[6], 5: w - z}
    t = COS45 * a[3]
    odd = {
        1: COS75 * a[1] + t + COS15 * a[5],
        3: COS45 * (a[1] + a[3] - a[5]),
        5: COS15 * a[1] - t + COS75 * a[5],
    }
    for k in (1, 3, 5):
        s[k], s[12 - k] = odd[k] + even[k], odd[k] - even[k]
    b = {j: o[j] - o[12 - j] for j in range(1, 6)}
    p1, p2 = b[1] + b[5], COS30 * (b[2] + b[4])
    w = 0.5 * p1 + b[3]
    s[2], s[6], s[10] = w + p2, p1 - b[3], w - p2
    p1, p2 = COS30 * (b[1] - b[5]), COS30 * (b[2] - b[4])
    s[4], s[8] = p1 + p2, p1 - p2

    out = [None] * 24
    out[0], out[12] = c[0], c[12]
    for k in range(1, 12):
        out[k], out[24 - k] = c[k] + s[k], c[k] - s[k]
    return out


def transform_rows(tiles, out_ref):
    for q in range(5):
        out = row_transform([tiles[q][8 * i : 8 * i + 8] for i in range(VDIM)])
        for i in range(VDIM):
            out_ref[q, 8 * i : 8 * i + 8, :] = out[i]


def row_image(ref, i):
    tiles = [ref[q, 8 * i : 8 * i + 8, :] for q in range(5)]
    return [*mixed(tiles[:4]), tiles[4]]


def collide_kernel(
    got_ref,
    one_ref,
    two_ref,
    place_ref,
    unplace_ref,
    gh_ref,
    gl_ref,
    ih_ref,
    il_ref,
    out_ref,
    flat_ref,
    x_ref,
    spectrum_ref,
    first_ref,
    second_ref,
    total_ref,
):
    for c in range(OWN):
        part = []
        for m in range(4):
            tiles = [got_ref[pl.ds(m * CHUNK + t * OWN + c, 8, stride=4 * CHUNK), :] for t in range(TILES)]
            part.append(jnp.concatenate([*tiles[:3], tiles[3][:, :TAIL]], axis=1))
        flat_ref[c * VDIM : c * VDIM + 8, :] = jnp.concatenate([part[0], part[1][:, :144]], axis=1)
        flat_ref[c * VDIM + 8 : c * VDIM + 16, :] = jnp.concatenate([part[1][:, 144:], part[2][:, :288]], axis=1)
        flat_ref[c * VDIM + 16 : c * VDIM + 24, :] = jnp.concatenate([part[2][:, 288:], part[3]], axis=1)
    high, low = split(flat_ref[...])
    placed = dot(high, place_ref[...]) + dot(low, place_ref[...])
    for c in range(OWN):
        for r in range(3):
            for q in range(5):
                value = placed[c * VDIM + 8 * r : c * VDIM + 8 * r + 8, q * LANES : (q + 1) * LANES]
                for copy in (0, OWN):
                    x_ref[q, pl.ds(8 * r + c + copy, 8, stride=VDIM), :] = value
    tiles = [x_ref[q] for q in range(5)]
    transform_rows(plane_product([*mixed(tiles[:4]), tiles[4]], gh_ref, gl_ref), spectrum_ref)

    upper = lax.broadcasted_iota(jnp.int32, (8, LANES), 0) < OWN

    def repeated(table_ref, i, t, q):
        return jnp.broadcast_to(table_ref[i, t : t + 1, q * LANES : (q + 1) * LANES], (8, LANES))

    def image(table_ref, top, bottom, out_ref):
        tiles = []
        for q in range(5):
            pieces = []
            for i in range(VDIM):
                table = repeated(table_ref, i, top, q)
                if bottom != top:
                    table = jnp.where(upper, table, repeated(table_ref, i, bottom, q))
                pieces.append(spectrum_ref[q, 8 * i : 8 * i + 8, :] * table)
            tiles.append(jnp.concatenate(pieces, axis=0))
        transform_rows(plane_product(tiles, ih_ref, il_ref), out_ref)

    for u in range(TERMS // 2):
        image(one_ref, 2 * u, 2 * u + 1, first_ref)
        image(two_ref, 2 * u, 2 * u + 1, second_ref)
        for i in range(VDIM):
            one, two = row_image(first_ref, i), row_image(second_ref, i)
            for q in range(5):
                at = slice(8 * i, 8 * i + 8)
                term = one[q] * two[q]
                total_ref[q, at, :] = term if u == 0 else total_ref[q, at, :] + term
    image(one_ref, TERMS, TERMS, first_ref)
    for i in range(VDIM):
        lost = row_image(first_ref, i)
        for q in range(5):
            at = slice(8 * i, 8 * i + 8)
            both = total_ref[q, at, :]
            total_ref[q, at, :] = both + pltpu.roll(both, OWN, 0) - x_ref[q, at, :] * lost[q]
    rows = [
        jnp.concatenate([total_ref[q, pl.ds(8 * r + c, 8, stride=VDIM), :] for q in range(5)], axis=1)
        for c in range(OWN)
        for r in range(3)
    ]
    high, low = split(jnp.concatenate(rows, axis=0))
    flat_ref[...] = dot(high, unplace_ref[...]) + dot(low, unplace_ref[...])
    for c in range(OWN):
        r0 = flat_ref[c * VDIM : c * VDIM + 8, :]
        r1 = flat_ref[c * VDIM + 8 : c * VDIM + 16, :]
        r2 = flat_ref[c * VDIM + 16 : c * VDIM + 24, :]
        part = [
            r0[:, :WIDTH],
            jnp.concatenate([r0[:, WIDTH:], r1[:, :288]], axis=1),
            jnp.concatenate([r1[:, 288:], r2[:, :144]], axis=1),
            r2[:, 144:],
        ]
        blank = jnp.zeros((8, LANES - TAIL), f32)
        for m in range(4):
            for t in range(TILES):
                piece = part[m][:, t * LANES : min((t + 1) * LANES, WIDTH)]
                if t == TILES - 1:
                    piece = jnp.concatenate([piece, blank], axis=1)
                out_ref[pl.ds(m * CHUNK + t * OWN + c, 8, stride=4 * CHUNK), :] = piece


SMALL = pl.BlockSpec(memory_space=pltpu.SMEM)
BIG = pl.BlockSpec(memory_space=pltpu.VMEM)
PARAMS = pltpu.CompilerParams(vmem_limit_bytes=48 * 1024 * 1024)


def shape(*dims):
    return jax.ShapeDtypeStruct(dims, f32)


def call(kernel, small, big, outs, scratch=(), name=None):
    return pl.pallas_call(
        kernel,
        out_shape=outs,
        in_specs=[SMALL] * len(small) + [BIG] * len(big),
        out_specs=jax.tree.map(lambda _: BIG, outs),
        scratch_shapes=list(scratch),
        compiler_params=PARAMS,
        name=name,
    )(*small, *big)


def swap_edges(edge):
    count = lax.axis_size("space")
    pair = [(i, i ^ 1) for i in range(count)]
    other = [(i, (((i + 1) ^ 1) - 1) % count) for i in range(count)]
    return lax.ppermute(edge, "space", pair), lax.ppermute(edge, "space", other)


def shards(
    distribution, neighbours, block_level, collide_mask, gain_first, gain_second, loss_rates
):
    pieces = hartley_pieces()
    tiles = shape(TILES, CELLS, LANES)
    edges = shape(7 * EDGE, LANES)
    packed = shape(GROUP * CHUNK, LANES)
    change = pltpu.VMEM((TILES, CELLS, LANES), f32)
    inner = shape(2, TILES, BSIDE, BSIDE, LANES)
    pick = jax.ShapeDtypeStruct((ACT, CELLS), bf16)
    mask = collide_mask.reshape(1, CELLS)
    scalars = [neighbours, block_level]
    rows = (5, VDIM * 2 * OWN, LANES)

    cells, edge = call(pack_kernel, [], [distribution.swapaxes(1, 2)], (tiles, edges), name="pack_edges")
    near = swap_edges(edge)
    inside, pick = call(inner_slots_kernel, [], [mask, cells], (inner, pick), name="first_inner")
    loss = loss_rates.reshape(1, -1)
    inside, loss = lax.optimization_barrier((inside, loss))
    one, edge_one = call(
        first_kernel, scalars, [cells, inside, edge, *near], (tiles, edges), [change], name="first_section"
    )
    near = swap_edges(edge_one)
    inside = call(inner_kernel, [], [one], inner, name="second_inner")
    table = (VDIM, 8, WIDE)
    tables = call(
        order_kernel,
        [],
        [gain_first, gain_second, loss, *pieces["order"]],
        (shape(*table), shape(*table)),
        [pltpu.VMEM(table, f32)] * 2,
        name="order_weights",
    )
    inside, tables = lax.optimization_barrier((inside, tables))
    two, send = call(
        second_kernel,
        scalars,
        [pick, cells, one, inside, edge_one, *near],
        (tiles, packed),
        [change],
        name="second_section",
    )
    got = lax.all_to_all(send, "vel", split_axis=0, concat_axis=0, tiled=True)
    collided = call(
        collide_kernel,
        [],
        [
            got,
            *tables,
            pieces["place"],
            pieces["unplace"],
            *pieces["plane_forward"],
            *pieces["plane_back"],
        ],
        packed,
        [pltpu.VMEM((OWN * VDIM, PLANE), f32)] + [pltpu.VMEM(rows, f32)] * 5,
        name="collide",
    )
    back = lax.all_to_all(collided, "vel", split_axis=0, concat_axis=0, tiled=True)
    total = pl.pallas_call(
        last_kernel,
        out_shape=shape(1, WIDTH, CELLS),
        in_specs=[BIG] * 3,
        out_specs=pl.BlockSpec(memory_space=pl.ANY),
        scratch_shapes=[pltpu.VMEM((TILES, LANES, CELLS), f32), pltpu.SemaphoreType.DMA((TILES,))],
        compiler_params=PARAMS,
        name="add_collision",
    )(pick, two, back)
    return total.swapaxes(1, 2)


def solution(mesh):
    in_specs = (P("space", None, "vel"), P("space", None), P("space"), P("space"), P(), P(), P())
    out_specs = P("space", None, "vel")
    return jax.shard_map(shards, mesh=mesh, in_specs=in_specs, out_specs=out_specs, check_vma=False)
```
